32 devices in a mesh: groups: 2 (over y), dp: 4 (over x, core), tensor: 4 (over z).
Axes of the slice: x: 2, y: 2, z: 4, core: 2. Of those that a mesh axis runs over, the one named last changes fastest.
Arguments:
- hidden: bfloat16 [6144, 8192], P(('groups', 'dp'), 'tensor'), parts along dimension 0, may hold values from -6 to 6
- query_weight: bfloat16 [8192, 8192], P(None, 'tensor'), may hold values from -0.0625 to 0.0625
- adapter_down: bfloat16 [32, 64, 8192], P('dp', None, 'tensor'), may hold values from -0.0625 to 0.0625
- adapter_up: bfloat16 [32, 64, 8192], P('dp', None, 'tensor'), may hold values from -0.75 to 0.75
- block_variant_index: int32 [8, 6], P('groups'), parts along dimension 0, may hold values from 0 to 31, as said below
- variant_pool_slot: int32 [64], P('groups'), parts along dimension 0, may hold values from 0 to 31, as said below
- block_live_count: int32 [8, 6], P(('groups', 'dp')), parts along dimension 0, may hold values from 1 to 128, 576 in all within a row
Outputs:
- query: bfloat16 [6144, 8192], P(('groups', 'dp'), 'tensor'), parts along dimension 0
The draws below stay inside these ranges and needn't reach their ends.
There are 2 independent parts, one for each index of `groups`. The reference program is written for one: setup_inputs(seed, part) draws one part's arguments, and reference() takes and returns one part's arrays. A program takes and returns all parts, laid end to end along the dimension named above; an argument that names none is the same for every part. Nothing has to cross between parts.
Inputs may be any that keep to these rules, and one draw needn't show every extreme that they name: variant_pool_slot is a permutation; variant v lies in pool slot variant_pool_slot[v], held by dp index variant_pool_slot[v] // 8. `block_variant_index`: let C be 6 divided by 4, rounded up; for each replica and each dp index, at most C of the replica's blocks name variants held by that index, and some index holds exactly C (so when 6 <= 4, a replica's blocks name variants on distinct dp indices). `block_live_count`: each replica's 6 counts sum to 576, and one of them is 128.
All inputs are finite; a program needn't handle non-finite values.
Results may differ from the reference program's by a relative error of at most 0.0045.
Values may be sent and summed in bfloat16 or wider, within the bound.
No kernel may reach another device: no remote copies, remote signals or barrier semaphores. Data moves between devices by JAX's collectives and lax.ppermute only.
A program may use at most 128 MiB of HBM per device.

```python
import math
import jax
import jax.numpy as jnp
import numpy as np

MODEL_WIDTH = 8192
QUERY_WIDTH = 8192
ADAPTER_RANK = 64
BLOCK_HEIGHT = 128
LIVE = 96
REPLICA_BLOCKS = 6
VAR_DEV = 8
SERVE_REPLICAS = 4
POOL_VARIANTS = 32
ROWS = 3072


def pool_layout(key):
    variant_pool_slot = jax.random.permutation(jax.random.fold_in(key, 101), POOL_VARIANTS).astype(jnp.int32)
    slot_capacity = (REPLICA_BLOCKS + SERVE_REPLICAS - 1) // SERVE_REPLICAS
    replica_keys = jax.random.split(jax.random.fold_in(key, 102), SERVE_REPLICAS)
    orders = jax.vmap(lambda k: jax.random.permutation(k, slot_capacity * SERVE_REPLICAS))(replica_keys)
    owners = (orders[:, :REPLICA_BLOCKS] // slot_capacity).astype(jnp.int32)
    local_slot = jax.random.randint(jax.random.fold_in(key, 103), (SERVE_REPLICAS, REPLICA_BLOCKS), 0, VAR_DEV).astype(jnp.int32)
    slots = owners * VAR_DEV + local_slot
    inverse = jnp.zeros((POOL_VARIANTS,), jnp.int32).at[variant_pool_slot].set(jnp.arange(POOL_VARIANTS, dtype=jnp.int32))
    return (variant_pool_slot, inverse[slots])


def draw_block_variant_index(key, part):
    return pool_layout(key)[1]


def draw_variant_pool_slot(key, part):
    return pool_layout(key)[0]


def block_levels(rng, shape, shards, low, largest):
    def one(axis_at, parts):
        steps = jax.random.uniform(jax.random.fold_in(jax.random.fold_in(rng, 6), axis_at), (parts,), jnp.float32, low / len(shards), largest / len(shards))
        return jnp.repeat(jnp.exp(steps), shape[axis_at] // parts).reshape((-1,) + (1,) * (len(shape) - axis_at - 1))

    level = one(*shards[0])
    for cut in shards[1:]:
        level = level * one(*cut)
    return level


def profile(count, total, limit, slope):
    weights = [(1 << 20) // math.isqrt(grade ** slope) + 1 for grade in range(2, count + 1)]
    surplus, holding = total - limit - (count - 1), [1] * (count - 1)
    while surplus > 0:
        free = [i for i in range(count - 1) if holding[i] < limit]
        whole, remaining = sum([weights[i] for i in free]), surplus
        for i in free:
            more = min(limit - holding[i], max(1, remaining * weights[i] // whole), surplus)
            holding[i] = holding[i] + more
            surplus = surplus - more
    return np.array([limit] + holding)


def ragged(own_key, amount, total, limit, slope):
    if amount == 2:
        one = jax.random.randint(own_key, (), max(1, total - limit), min(limit, total - 1) + 1)
        return jnp.stack([one, total - one])
    lengths = jnp.asarray(profile(amount, total, limit, slope), jnp.int32)
    pairs = (amount - 1) // 2
    giver, receiver = lengths[1:1 + 2 * pairs:2], lengths[2:2 + 2 * pairs:2]
    slack = jnp.minimum(giver - 1, limit - receiver)
    passed = jax.random.randint(jax.random.fold_in(own_key, 1), (pairs,), 0, 1 << 20) % (slack + 1)
    lengths = lengths.at[1:1 + 2 * pairs:2].set(giver - passed).at[2:2 + 2 * pairs:2].set(receiver + passed)
    return lengths[jax.random.permutation(jax.random.fold_in(own_key, 2), amount)]


def scatter_about(own_key, dims, width, most, shards=(), kind=jnp.bfloat16):
    loudness = block_levels(own_key, dims, shards, -0.22, 0.18) if shards else 1.0
    values = jax.random.normal(own_key, dims, jnp.float32) * width * loudness
    return jnp.minimum(jnp.maximum(values, -most), most).astype(kind)


def setup_inputs(seed: int = 0, part: int = 0) -> dict:
    seeds = jax.random.split(jax.random.key(seed), 8)
    own_keys = jax.random.split(jax.random.fold_in(seeds[7], part), 8)
    hidden = scatter_about(own_keys[0], (ROWS, MODEL_WIDTH), 1.0, 6.0, ((0, 4), (1, 4)))
    query_weight = scatter_about(seeds[1], (MODEL_WIDTH, QUERY_WIDTH), MODEL_WIDTH ** -0.5, 0.0625, ((1, 4),))
    adapter_down = scatter_about(seeds[2], (POOL_VARIANTS, ADAPTER_RANK, MODEL_WIDTH), MODEL_WIDTH ** -0.5, 0.0625, ((0, 4), (2, 4)))
    adapter_up = scatter_about(seeds[3], (POOL_VARIANTS, ADAPTER_RANK, QUERY_WIDTH), ADAPTER_RANK ** -0.5, 0.75, ((0, 4), (2, 4)))
    block_variant_index = draw_block_variant_index(jax.random.fold_in(jax.random.fold_in(seeds[7], part), 71), part)
    variant_pool_slot = draw_variant_pool_slot(jax.random.fold_in(jax.random.fold_in(seeds[7], part), 71), part)
    block_live_count = jax.vmap(lambda own: ragged(own, REPLICA_BLOCKS, LIVE * REPLICA_BLOCKS, BLOCK_HEIGHT, 2))(jax.random.split(own_keys[6], SERVE_REPLICAS)).reshape((SERVE_REPLICAS, REPLICA_BLOCKS)).astype(jnp.int32)
    return {"hidden": hidden, "query_weight": query_weight, "adapter_down": adapter_down, "adapter_up": adapter_up, "block_variant_index": block_variant_index, "variant_pool_slot": variant_pool_slot, "block_live_count": block_live_count}


adapter_scale = 2.0


def reference(hidden, query_weight, adapter_down, adapter_up, block_variant_index, variant_pool_slot, block_live_count):
    base_output = jnp.dot(hidden, query_weight, preferred_element_type=jnp.float32)
    slots_per_block = variant_pool_slot[block_variant_index].reshape(-1).astype(jnp.int32)
    picked_down_factor = jnp.take(adapter_down, slots_per_block, axis=0).astype(jnp.float32)
    picked_up_factor = jnp.take(adapter_up, slots_per_block, axis=0).astype(jnp.float32)
    blocked = hidden.reshape(SERVE_REPLICAS * REPLICA_BLOCKS, BLOCK_HEIGHT, MODEL_WIDTH).astype(jnp.float32)
    down_projected = jnp.einsum("nrd,nkd->nrk", blocked, picked_down_factor).astype(jnp.bfloat16)
    adapter_delta = jnp.einsum("bls,bsm->blm", down_projected.astype(jnp.float32), picked_up_factor)
    live_mask = jnp.arange(BLOCK_HEIGHT)[None, :] < block_live_count.reshape(-1)[:, None]
    reduced_sum = base_output.reshape(SERVE_REPLICAS * REPLICA_BLOCKS, BLOCK_HEIGHT, QUERY_WIDTH) + adapter_scale * adapter_delta
    result = jnp.where(live_mask[:, :, None], reduced_sum, jnp.float32(0.0))
    return result.reshape(ROWS, QUERY_WIDTH).astype(jnp.bfloat16)
```

```python
import jax
import jax.numpy as jnp
from jax import lax
from jax.sharding import PartitionSpec as P

adapter_scale = 2.0
live_total = 576
feature_chunks = 4


def shift(x, axis, step, size):
    pairs = [(i, i + step) for i in range(size) if 0 <= i + step < size]
    return lax.ppermute(x, axis, pairs)


def shards(
    hidden,
    query_weight,
    adapter_down,
    adapter_up,
    block_variant_index,
    variant_pool_slot,
    block_live_count,
):
    replicas = lax.axis_size("dp")
    replica = lax.axis_index("dp")
    tensor = lax.axis_size("tensor")
    pool = adapter_down.shape[0]
    blocks = block_variant_index.shape[1]
    rows, width = hidden.shape
    block = rows // blocks
    rank = adapter_down.shape[1]
    columns = query_weight.shape[1]
    capacity = (blocks + replicas - 1) // replicas
    bf16, f32 = jnp.bfloat16, jnp.float32

    live = block_live_count[0]
    start = jnp.cumsum(live) - live
    row = jnp.arange(rows)
    inside = row % block
    is_live = inside < jnp.repeat(live, block)
    place = jnp.where(is_live, jnp.repeat(start, block) + inside, -1)
    pack = (jnp.arange(live_total)[:, None] == place[None, :]).astype(bf16)
    packed = jnp.dot(pack, hidden, preferred_element_type=f32).astype(bf16)

    piece = width // feature_chunks
    gathered = [
        lax.all_gather(packed[:, j * piece : (j + 1) * piece], "tensor", axis=0)
        for j in range(feature_chunks)
    ]

    slots = variant_pool_slot[block_variant_index]
    owners = slots // pool
    local = slots % pool
    earlier = jnp.arange(blocks)[None, :] < jnp.arange(blocks)[:, None]
    nth = jnp.sum(
        ((owners[:, :, None] == owners[:, None, :]) & earlier[None]).astype(jnp.int32), axis=2
    )

    def outgoing(target):
        o, l, m = owners[target], local[target], nth[target]
        hit = (o[None, :] == replica) & (m[None, :] == jnp.arange(capacity)[:, None])
        index = jnp.sum(jnp.where(hit, l[None, :], 0), axis=1)
        return jnp.take(adapter_down, index, axis=0), jnp.take(adapter_up, index, axis=0)

    downs, ups = [], []
    for step in range(replicas):
        target = (replica + step) % replicas
        d, u = outgoing(target)
        if step:
            pairs = [(i, (i + step) % replicas) for i in range(replicas)]
            d = lax.ppermute(d, "dp", pairs)
            u = lax.ppermute(u, "dp", pairs)
        downs.append(d)
        ups.append(u)
    groups = replicas * capacity
    down_all = jnp.concatenate(downs, axis=0).reshape(groups * rank, width)
    up_all = jnp.concatenate(ups, axis=0).reshape(groups * rank, columns)

    my_owner, my_nth = owners[replica], nth[replica]
    my_group = ((replica - my_owner) % replicas) * capacity + my_nth
    live_row = jnp.arange(live_total)
    row_block = jnp.sum((live_row[:, None] >= start[None, :]).astype(jnp.int32), axis=1) - 1
    row_group = jnp.sum(
        jnp.where(row_block[:, None] == jnp.arange(blocks)[None, :], my_group[None, :], 0), axis=1
    )
    mask = row_group[:, None] == jnp.arange(groups)[None, :]

    wide = lax.dot_general(
        packed, down_all, (((1,), (1,)), ((), ())), preferred_element_type=f32
    ).reshape(live_total, groups, rank)
    partial = jnp.sum(jnp.where(mask[:, :, None], wide, 0.0), axis=1)

    before, after = jnp.zeros_like(partial), jnp.zeros_like(partial)
    for _ in range(tensor - 1):
        before = shift(partial + before, "tensor", 1, tensor)
        after = shift(partial + after, "tensor", -1, tensor)
    shrink = (before + partial + after).astype(bf16)
    spread = jnp.where(
        mask[:, :, None], (shrink * bf16(adapter_scale))[:, None, :], bf16(0.0)
    ).reshape(live_total, groups * rank)

    total = jnp.dot(spread, up_all, preferred_element_type=f32)
    weight = query_weight.reshape(tensor, feature_chunks, piece, columns)
    for j in range(feature_chunks):
        for t in range(tensor):
            total = total + jnp.dot(gathered[j][t], weight[t, j], preferred_element_type=f32)
    result = total.astype(bf16)
    unpack = (place[:, None] == jnp.arange(live_total)[None, :]).astype(bf16)
    return jnp.dot(unpack, result, preferred_element_type=f32).astype(bf16)


def solution(mesh):
    return jax.shard_map(
        shards,
        mesh=mesh,
        in_specs=(
            P(("groups", "dp"), "tensor"),
            P(None, "tensor"),
            P("dp", None, "tensor"),
            P("dp", None, "tensor"),
            P("groups", None),
            P("groups"),
            P(("groups", "dp"), None),
        ),
        out_specs=P(("groups", "dp"), "tensor"),
        check_vma=False,
    )
```

```python
import functools

import jax
import jax.numpy as jnp
from jax import lax
from jax.experimental import pallas as pl
from jax.experimental.pallas import tpu as pltpu
from jax.sharding import PartitionSpec as P

adapter_scale = 2.0
live_total = 576
chunk_width = 1024
column_tile = 512
vmem_bytes = 48 * 1024 * 1024
bf16, f32, i32 = jnp.bfloat16, jnp.float32, jnp.int32

smem = pl.BlockSpec(memory_space=pltpu.SMEM)
hbm = pl.BlockSpec(memory_space=pl.ANY)


def params():
    return pltpu.CompilerParams(vmem_limit_bytes=vmem_bytes)


def cost(flops, moved):
    return pl.CostEstimate(flops=int(flops), bytes_accessed=int(moved), transcendentals=0)


def shift(x, axis, step, size, first, last):
    pairs = [(i, i + step) for i in range(first, last + 1) if 0 <= i + step < size]
    return lax.ppermute(x, axis, pairs)


def one_hot(live, rows, axis):
    blocks = live.shape[1]
    block = rows // blocks
    flat = (1, rows) if axis else (rows, 1)
    row = lax.broadcasted_iota(i32, flat, axis)
    place = jnp.full(flat, -1, i32)
    start = 0
    for b in range(blocks):
        inside = row - b * block
        here = (inside >= 0) & (inside < live[0, b])
        place = jnp.where(here, inside + start, place)
        start = start + live[0, b]
    shape = (live_total, rows) if axis else (rows, live_total)
    return (lax.broadcasted_iota(i32, shape, 1 - axis) == place).astype(f32).astype(bf16)


def pack_kernel(live, x, out):
    hot = one_hot(live, x.shape[0], 1)
    out[...] = jnp.dot(hot, x[...], preferred_element_type=f32).astype(bf16)


def pack(hidden, live, j, piece):
    rows = hidden.shape[0]
    return pl.pallas_call(
        pack_kernel,
        grid=(1,),
        in_specs=[smem, pl.BlockSpec((rows, piece), lambda i: (0, j))],
        out_specs=pl.BlockSpec((live_total, piece), lambda i: (0, 0)),
        out_shape=jax.ShapeDtypeStruct((live_total, piece), bf16),
        compiler_params=params(),
        cost_estimate=cost(2 * rows * live_total * piece, (rows + live_total) * piece * 2),
        name="pack",
    )(live, hidden)


def choose_kernel(variants, slots, down, up, *rest, replicas, capacity, blocks):
    outs, sems = rest[:replicas], rest[replicas]
    pool, rank = down.shape[0], down.shape[1]
    me = lax.axis_index("dp")
    copies = []
    for step in range(replicas):
        target = lax.rem(me + step, replicas)
        seen = jnp.int32(0)
        index = [jnp.int32(0)] * capacity
        for b in range(blocks):
            slot = slots[variants[target, b]]
            owner = lax.div(slot, pool)
            mine = owner == me
            for m in range(capacity):
                index[m] = jnp.where(mine & (seen == m), slot - owner * pool, index[m])
            seen = seen + mine.astype(i32)
        for m in range(capacity):
            for kind, source in enumerate((down, up)):
                copies.append(
                    pltpu.make_async_copy(
                        source.at[index[m]],
                        outs[step].at[kind, m * rank : (m + 1) * rank],
                        sems.at[len(copies)],
                    )
                )
                copies[-1].start()
    for copy in copies:
        copy.wait()


def choose(variants, slots, down, up, replicas, capacity):
    pool, rank, width = down.shape
    out = jax.ShapeDtypeStruct((2, capacity * rank, width), bf16)
    return pl.pallas_call(
        functools.partial(
            choose_kernel, replicas=replicas, capacity=capacity, blocks=variants.shape[1]
        ),
        in_specs=[smem, smem, hbm, hbm],
        out_specs=[hbm] * replicas,
        out_shape=[out] * replicas,
        scratch_shapes=[pltpu.SemaphoreType.DMA((replicas * capacity * 2,))],
        compiler_params=params(),
        cost_estimate=cost(0, replicas * capacity * rank * width * 8),
        name="choose",
    )(variants, slots, down, up)


def row_groups(variants, slots, live, shape, axis, replicas, capacity, pool):
    me = lax.axis_index("dp")
    blocks = live.shape[1]
    row = lax.broadcasted_iota(i32, shape, axis)
    group = jnp.zeros(shape, i32)
    start = 0
    owners = []
    for b in range(blocks):
        owner = lax.div(slots[variants[me, b]], pool)
        nth = sum([(o == owner).astype(i32) for o in owners], jnp.int32(0))
        owners.append(owner)
        mine = lax.rem(me - owner + replicas, replicas) * capacity + nth
        group = jnp.where(row >= start, mine, group)
        start = start + live[0, b]
    return group


def shrink_kernel(variants, slots, live, *rest, replicas, capacity, pool, chunks):
    xs, downs, out = rest[:chunks], rest[chunks : chunks + replicas], rest[-1]
    depth = downs[0].shape[1]
    rank = out.shape[0]
    piece = xs[0].shape[1]
    shape = (depth, live_total)
    group = row_groups(variants, slots, live, shape, 1, replicas, capacity, pool)
    nth = lax.broadcasted_iota(i32, shape, 0) // rank
    total = jnp.zeros(shape, f32)
    for o in range(replicas):
        part = jnp.zeros(shape, f32)
        for j in range(chunks):
            part = part + lax.dot_general(
                downs[o][0, :, j * piece : (j + 1) * piece],
                xs[j][...],
                (((1,), (1,)), ((), ())),
                preferred_element_type=f32,
            )
        total = total + jnp.where(group == o * capacity + nth, part, 0.0)
    result = total[:rank]
    for m in range(1, capacity):
        result = result + total[m * rank : (m + 1) * rank]
    out[...] = result


def shrink(variants, slots, live, xs, factors, capacity, pool):
    replicas = len(factors)
    depth, width = factors[0].shape[1:]
    rank = depth // capacity
    whole = pl.BlockSpec(memory_space=pltpu.VMEM)
    down = pl.BlockSpec((1, depth, width), lambda i: (0, 0, 0))
    return pl.pallas_call(
        functools.partial(
            shrink_kernel, replicas=replicas, capacity=capacity, pool=pool, chunks=len(xs)
        ),
        grid=(1,),
        in_specs=[smem] * 3
        + [pl.BlockSpec(x.shape, lambda i: (0, 0)) for x in xs]
        + [down] * replicas,
        out_specs=pl.BlockSpec((rank, live_total), lambda i: (0, 0)),
        out_shape=jax.ShapeDtypeStruct((rank, live_total), f32),
        compiler_params=params(),
        cost_estimate=cost(
            2 * live_total * width * depth * replicas, (live_total + depth * replicas) * width * 2
        ),
        name="shrink",
    )(variants, slots, live, *xs, *factors)


def project_kernel(*refs, count, has_total, delta, last, replicas, capacity, pool):
    refs = list(refs)
    meta = refs.pop(0)
    variants, slots, live = refs[:3]
    refs = refs[3:]
    total = refs.pop(0) if has_total else None
    xs, ws = refs[:count], refs[count : 2 * count]
    refs = refs[2 * count :]
    if delta:
        low, ups = refs[0], refs[1 : 1 + replicas]
        refs = refs[1 + replicas :]
    out = refs.pop(0)
    held = refs.pop(0) if last else out

    if has_total:
        held[...] = total[...]
    else:
        held[...] = jnp.zeros(held.shape, f32)
    for s in range(count):

        @pl.when(meta[2 * s + 1] > 0)
        def _(s=s):
            held[...] += jnp.dot(xs[s][...], ws[s][...], preferred_element_type=f32)

    if delta:
        depth = ups[0].shape[1]
        shape = (live_total, depth)
        group = row_groups(variants, slots, live, shape, 0, replicas, capacity, pool)
        nth = lax.broadcasted_iota(i32, shape, 1) // (depth // capacity)
        wide = jnp.concatenate([low[...]] * capacity, axis=1) * adapter_scale
        for o in range(replicas):
            spread = jnp.where(group == o * capacity + nth, wide, 0.0).astype(bf16)
            held[...] += jnp.dot(spread, ups[o][0], preferred_element_type=f32)
    if last:
        hot = one_hot(live, out.shape[0], 0)
        result = held[...].astype(bf16)
        out[...] = jnp.dot(hot, result, preferred_element_type=f32).astype(bf16)


def project(meta, ints, total, xs, weight, sizes, low=None, factors=None, rows=None):
    replicas, capacity, pool = sizes
    columns = weight.shape[1]
    tile = min(column_tile, columns)
    count = len(xs)
    in_specs = [smem] * 3
    args = list(ints)
    if total is not None:
        in_specs.append(pl.BlockSpec((live_total, tile), lambda i, m: (0, i)))
        args.append(total)
    for x in xs:
        in_specs.append(pl.BlockSpec(x.shape, lambda i, m: (0, 0)))
        args.append(x)
    for s, x in enumerate(xs):
        in_specs.append(pl.BlockSpec((x.shape[1], tile), lambda i, m, s=s: (m[2 * s], i)))
        args.append(weight)
    flops = sum(2 * live_total * x.shape[1] * columns for x in xs)
    moved = sum(x.size * 2 + x.shape[1] * columns * 2 for x in xs) + live_total * columns * 8
    if low is not None:
        in_specs.append(pl.BlockSpec(low.shape, lambda i, m: (0, 0)))
        args.append(low)
        for u in factors:
            in_specs.append(pl.BlockSpec((1, u.shape[1], tile), lambda i, m: (1, 0, i)))
            args.append(u)
            flops += 2 * live_total * u.shape[1] * columns
    scratch = []
    if rows is None:
        out = jax.ShapeDtypeStruct((live_total, columns), f32)
        out_spec = pl.BlockSpec((live_total, tile), lambda i, m: (0, i))
    else:
        out = jax.ShapeDtypeStruct((rows, columns), bf16)
        out_spec = pl.BlockSpec((rows, tile), lambda i, m: (0, i))
        scratch = [pltpu.VMEM((live_total, tile), f32)]
    return pl.pallas_call(
        functools.partial(
            project_kernel,
            count=count,
            has_total=total is not None,
            delta=low is not None,
            last=rows is not None,
            replicas=replicas,
            capacity=capacity,
            pool=pool,
        ),
        grid_spec=pltpu.PrefetchScalarGridSpec(
            num_scalar_prefetch=1,
            grid=(columns // tile,),
            in_specs=in_specs,
            out_specs=out_spec,
            scratch_shapes=scratch,
        ),
        out_shape=out,
        compiler_params=params(),
        cost_estimate=cost(flops, moved),
        name="project",
    )(meta, *args)


def shards(
    hidden,
    query_weight,
    adapter_down,
    adapter_up,
    block_variant_index,
    variant_pool_slot,
    block_live_count,
):
    replicas = lax.axis_size("dp")
    tensor = lax.axis_size("tensor")
    place = lax.axis_index("tensor")
    pool = adapter_down.shape[0]
    blocks = block_variant_index.shape[1]
    rows, width = hidden.shape
    capacity = (blocks + replicas - 1) // replicas
    piece = min(chunk_width, width)
    chunks = width // piece
    ints = (block_variant_index, variant_pool_slot, block_live_count)
    sizes = (replicas, capacity, pool)

    own = [pack(hidden, block_live_count, j, piece) for j in range(chunks)]

    right, left = [own], [own]
    for step in range(1, tensor):
        right.append([shift(x, "tensor", 1, tensor, step - 1, tensor - 2) for x in right[-1]])
        left.append([shift(x, "tensor", -1, tensor, 1, tensor - step) for x in left[-1]])

    factors = choose(block_variant_index, variant_pool_slot, adapter_down, adapter_up, replicas, capacity)
    got = [factors[0]]
    for step in range(1, replicas):
        pairs = [(i, (i + step) % replicas) for i in range(replicas)]
        got.append(lax.ppermute(factors[step], "dp", pairs))
    partial = shrink(*ints, own, got, capacity, pool)
    before, after = jnp.zeros_like(partial), jnp.zeros_like(partial)
    for step in range(1, tensor):
        before = lax.ppermute(partial + before, "tensor", [(i, i + 1) for i in range(tensor - 1)])
        after = lax.ppermute(partial + after, "tensor", [(i, i - 1) for i in range(1, tensor)])
    low = (before + partial + after).astype(bf16).astype(f32).T

    def meta(items):
        pairs = []
        for source, j in items:
            there = (source >= 0) & (source < tensor)
            pairs += [jnp.clip(source, 0, tensor - 1) * chunks + j, there.astype(i32)]
        return jnp.stack([jnp.asarray(p, i32) for p in pairs])

    items = [(place, j) for j in range(chunks)]
    total = project(meta(items), ints, None, own, query_weight, sizes)
    for step in range(1, tensor):
        pieces = [range(chunks)] if step < tensor - 1 else [[j] for j in range(chunks)]
        for js in pieces:
            items = [(place - step, j) for j in js] + [(place + step, j) for j in js]
            xs = [right[step][j] for j in js] + [left[step][j] for j in js]
            final = step == tensor - 1 and js[-1] == chunks - 1
            with_delta = step == tensor - 1 and js[0] == 0
            total = project(
                meta(items),
                ints,
                total,
                xs,
                query_weight,
                sizes,
                low if with_delta else None,
                got if with_delta else None,
                rows if final else None,
            )
    return total


def solution(mesh):
    return jax.shard_map(
        shards,
        mesh=mesh,
        in_specs=(
            P(("groups", "dp"), "tensor"),
            P(None, "tensor"),
            P("dp", None, "tensor"),
            P("dp", None, "tensor"),
            P("groups", None),
            P("groups"),
            P(("groups", "dp"), None),
        ),
        out_specs=P(("groups", "dp"), "tensor"),
        check_vma=False,
    )
```

```python
import functools

import jax
import jax.numpy as jnp
from jax import lax
from jax.experimental import pallas as pl
from jax.experimental.pallas import tpu as pltpu
from jax.sharding import PartitionSpec as P

adapter_scale = 2.0
live_total = 576
tail_width = 256
column_tile = 512
vmem_bytes = 48 * 1024 * 1024
bf16, f32, i32 = jnp.bfloat16, jnp.float32, jnp.int32

smem = pl.BlockSpec(memory_space=pltpu.SMEM)
hbm = pl.BlockSpec(memory_space=pl.ANY)


def params():
    return pltpu.CompilerParams(vmem_limit_bytes=vmem_bytes)


def cost(flops, moved):
    return pl.CostEstimate(flops=int(flops), bytes_accessed=int(moved), transcendentals=0)


def one_hot(live, rows, axis):
    blocks = live.shape[1]
    block = rows // blocks
    flat = (1, rows) if axis else (rows, 1)
    row = lax.broadcasted_iota(i32, flat, axis)
    place = jnp.full(flat, -1, i32)
    start = 0
    for b in range(blocks):
        inside = row - b * block
        here = (inside >= 0) & (inside < live[0, b])
        place = jnp.where(here, inside + start, place)
        start = start + live[0, b]
    shape = (live_total, rows) if axis else (rows, live_total)
    return (lax.broadcasted_iota(i32, shape, 1 - axis) == place).astype(f32).astype(bf16)


def pack_kernel(live, x, *outs):
    hot = one_hot(live, x.shape[0], 1)
    start = 0
    for out in outs:
        stop = start + out.shape[1]
        rows = jnp.dot(hot, x[:, start:stop], preferred_element_type=f32)
        out[...] = rows.astype(bf16)
        start = stop


def pack(hidden, live, widths):
    rows, width = hidden.shape
    return pl.pallas_call(
        pack_kernel,
        grid=(1,),
        in_specs=[smem, pl.BlockSpec((rows, width), lambda i: (0, 0))],
        out_specs=[pl.BlockSpec((live_total, w), lambda i: (0, 0)) for w in widths],
        out_shape=[jax.ShapeDtypeStruct((live_total, w), bf16) for w in widths],
        compiler_params=params(),
        cost_estimate=cost(2 * rows * live_total * width, (rows + live_total) * width * 2),
        name="pack",
    )(live, hidden)


def choose_kernel(variants, slots, down, up, *rest, replicas, capacity, blocks):
    outs, sems = rest[:replicas], rest[replicas]
    pool, rank = down.shape[0], down.shape[1]
    me = lax.axis_index("dp")
    copies = []
    for step in range(replicas):
        target = lax.rem(me + step, replicas)
        seen = jnp.int32(0)
        index = [jnp.int32(0)] * capacity
        for b in range(blocks):
            slot = slots[variants[target, b]]
            owner = lax.div(slot, pool)
            mine = owner == me
            for m in range(capacity):
                index[m] = jnp.where(mine & (seen == m), slot - owner * pool, index[m])
            seen = seen + mine.astype(i32)
        for m in range(capacity):
            for kind, source in enumerate((down, up)):
                copies.append(
                    pltpu.make_async_copy(
                        source.at[index[m]],
                        outs[step].at[kind, m * rank : (m + 1) * rank],
                        sems.at[len(copies)],
                    )
                )
                copies[-1].start()
    for copy in copies:
        copy.wait()


def choose(variants, slots, down, up, replicas, capacity):
    pool, rank, width = down.shape
    out = jax.ShapeDtypeStruct((2, capacity * rank, width), bf16)
    return pl.pallas_call(
        functools.partial(
            choose_kernel, replicas=replicas, capacity=capacity, blocks=variants.shape[1]
        ),
        in_specs=[smem, smem, hbm, hbm],
        out_specs=[hbm] * replicas,
        out_shape=[out] * replicas,
        scratch_shapes=[pltpu.SemaphoreType.DMA((replicas * capacity * 2,))],
        compiler_params=params(),
        cost_estimate=cost(0, replicas * capacity * rank * width * 8),
        name="choose",
    )(variants, slots, down, up)


def row_groups(variants, slots, live, shape, axis, replicas, capacity, pool):
    me = lax.axis_index("dp")
    blocks = live.shape[1]
    row = lax.broadcasted_iota(i32, shape, axis)
    group = jnp.zeros(shape, i32)
    start = 0
    owners = []
    for b in range(blocks):
        owner = lax.div(slots[variants[me, b]], pool)
        nth = sum([(o == owner).astype(i32) for o in owners], jnp.int32(0))
        owners.append(owner)
        mine = lax.rem(me - owner + replicas, replicas) * capacity + nth
        group = jnp.where(row >= start, mine, group)
        start = start + live[0, b]
    return group


def shrink_kernel(variants, slots, live, *rest, replicas, capacity, pool, chunks):
    xs, downs, out = rest[:chunks], rest[chunks : chunks + replicas], rest[-1]
    depth = downs[0].shape[1]
    rank = out.shape[0]
    shape = (depth, live_total)
    group = row_groups(variants, slots, live, shape, 1, replicas, capacity, pool)
    nth = lax.broadcasted_iota(i32, shape, 0) // rank
    total = jnp.zeros(shape, f32)
    for o in range(replicas):
        part = jnp.zeros(shape, f32)
        start = 0
        for x in xs:
            stop = start + x.shape[1]
            part = part + lax.dot_general(
                downs[o][0, :, start:stop],
                x[...],
                (((1,), (1,)), ((), ())),
                preferred_element_type=f32,
            )
            start = stop
        total = total + jnp.where(group == o * capacity + nth, part, 0.0)
    result = total[:rank]
    for m in range(1, capacity):
        result = result + total[m * rank : (m + 1) * rank]
    out[...] = result


def shrink(variants, slots, live, xs, factors, capacity, pool):
    replicas = len(factors)
    depth, width = factors[0].shape[1:]
    rank = depth // capacity
    whole = pl.BlockSpec(memory_space=pltpu.VMEM)
    down = pl.BlockSpec((1, depth, width), lambda i: (0, 0, 0))
    return pl.pallas_call(
        functools.partial(
            shrink_kernel, replicas=replicas, capacity=capacity, pool=pool, chunks=len(xs)
        ),
        grid=(1,),
        in_specs=[smem] * 3
        + [pl.BlockSpec(x.shape, lambda i: (0, 0)) for x in xs]
        + [down] * replicas,
        out_specs=pl.BlockSpec((rank, live_total), lambda i: (0, 0)),
        out_shape=jax.ShapeDtypeStruct((rank, live_total), f32),
        compiler_params=params(),
        cost_estimate=cost(
            2 * live_total * width * depth * replicas, (live_total + depth * replicas) * width * 2
        ),
        name="shrink",
    )(variants, slots, live, *xs, *factors)


def near_kernel(meta, variants, slots, live, x, w, low, *rest, replicas, capacity, pool):
    ups, out = rest[:replicas], rest[replicas]
    depth = ups[0].shape[1]
    shape = (live_total, depth)
    group = row_groups(variants, slots, live, shape, 0, replicas, capacity, pool)
    nth = lax.broadcasted_iota(i32, shape, 1) // (depth // capacity)
    wide = jnp.concatenate([low[...]] * capacity, axis=1) * adapter_scale
    total = jnp.dot(x[...], w[0], preferred_element_type=f32)
    for o in range(replicas):
        spread = jnp.where(group == o * capacity + nth, wide, 0.0).astype(bf16)
        total = total + jnp.dot(spread, ups[o][0], preferred_element_type=f32)
    out[...] = total


def near(meta, ints, x, weight, low, factors, sizes):
    replicas, capacity, pool = sizes
    columns = weight.shape[2]
    tile = min(column_tile, columns)
    depth = factors[0].shape[1]
    k = x.shape[1]
    return pl.pallas_call(
        functools.partial(near_kernel, replicas=replicas, capacity=capacity, pool=pool),
        grid_spec=pltpu.PrefetchScalarGridSpec(
            num_scalar_prefetch=1,
            grid=(columns // tile,),
            in_specs=[smem] * 3
            + [
                pl.BlockSpec(x.shape, lambda i, m: (0, 0)),
                pl.BlockSpec((1, k, tile), lambda i, m: (m[0], 0, i)),
                pl.BlockSpec(low.shape, lambda i, m: (0, 0)),
            ]
            + [pl.BlockSpec((1, depth, tile), lambda i, m: (1, 0, i))] * replicas,
            out_specs=pl.BlockSpec((live_total, tile), lambda i, m: (0, i)),
        ),
        out_shape=jax.ShapeDtypeStruct((live_total, columns), f32),
        compiler_params=params(),
        cost_estimate=cost(
            2 * live_total * columns * (k + replicas * depth), columns * (k * 2 + live_total * 4)
        ),
        name="near",
    )(meta, *ints, x, weight, low, *factors)


def far_kernel(meta, total, x, w, out):
    @pl.when(pl.program_id(0) == 0)
    def _():
        out[...] = total[...]

    out[...] += jnp.dot(x[0], w[0], preferred_element_type=f32)


def far(meta, total, x, weight):
    tensor, _, k = x.shape
    columns = weight.shape[2]
    return pl.pallas_call(
        far_kernel,
        grid_spec=pltpu.PrefetchScalarGridSpec(
            num_scalar_prefetch=1,
            grid=(tensor - 1,),
            in_specs=[
                pl.BlockSpec((live_total, columns), lambda i, m: (0, 0)),
                pl.BlockSpec((1, live_total, k), lambda i, m: (m[1 + i], 0, 0)),
                pl.BlockSpec((1, k, columns), lambda i, m: (m[1 + i], 0, 0)),
            ],
            out_specs=pl.BlockSpec((live_total, columns), lambda i, m: (0, 0)),
        ),
        out_shape=jax.ShapeDtypeStruct((live_total, columns), f32),
        compiler_params=params(),
        cost_estimate=cost(
            2 * live_total * columns * k * (tensor - 1), tensor * k * (columns + live_total) * 2
        ),
        name="far",
    )(meta, total, x, weight)


def finish_kernel(live, total, x, w, out, hot):
    @pl.when(pl.program_id(0) == 0)
    def _():
        hot[...] = one_hot(live, out.shape[0], 0)

    result = total[...]
    for t in range(x.shape[0]):
        result = result + jnp.dot(x[t], w[t], preferred_element_type=f32)
    rows = jnp.dot(hot[...], result.astype(bf16), preferred_element_type=f32)
    out[...] = rows.astype(bf16)


def finish(live, total, x, weight, rows):
    tensor, _, k = x.shape
    columns = weight.shape[2]
    tile = min(column_tile, columns)
    last = weight.shape[1] // k - 1
    return pl.pallas_call(
        finish_kernel,
        grid=(columns // tile,),
        in_specs=[
            smem,
            pl.BlockSpec((live_total, tile), lambda i: (0, i)),
            pl.BlockSpec((tensor, live_total, k), lambda i: (0, 0, 0)),
            pl.BlockSpec((tensor, k, tile), lambda i: (0, last, i)),
        ],
        out_specs=pl.BlockSpec((rows, tile), lambda i: (0, i)),
        out_shape=jax.ShapeDtypeStruct((rows, columns), bf16),
        scratch_shapes=[pltpu.VMEM((rows, live_total), bf16)],
        compiler_params=params(),
        cost_estimate=cost(
            2 * live_total * columns * (k * tensor + rows), columns * (live_total * 4 + rows * 2)
        ),
        name="finish",
    )(live, total, x, weight)


def shards(
    hidden,
    query_weight,
    adapter_down,
    adapter_up,
    block_variant_index,
    variant_pool_slot,
    block_live_count,
):
    replicas = lax.axis_size("dp")
    tensor = lax.axis_size("tensor")
    place = lax.axis_index("tensor")
    pool = adapter_down.shape[0]
    blocks = block_variant_index.shape[1]
    rows, width = hidden.shape
    capacity = (blocks + replicas - 1) // replicas
    tail = min(tail_width, width // 2)
    ints = (block_variant_index, variant_pool_slot, block_live_count)
    sizes = (replicas, capacity, pool)

    own = pack(hidden, block_live_count, (width - tail, tail))
    gathered = [lax.all_gather(x, "tensor", axis=0) for x in own]

    factors = choose(block_variant_index, variant_pool_slot, adapter_down, adapter_up, replicas, capacity)
    got = [factors[0]]
    for step in range(1, replicas):
        pairs = [(i, (i + step) % replicas) for i in range(replicas)]
        got.append(lax.ppermute(factors[step], "dp", pairs))

    partial = shrink(*ints, own, got, capacity, pool)
    before, after = jnp.zeros_like(partial), jnp.zeros_like(partial)
    for step in range(1, tensor):
        before = lax.ppermute(partial + before, "tensor", [(i, i + 1) for i in range(tensor - 1)])
        after = lax.ppermute(partial + after, "tensor", [(i, i - 1) for i in range(1, tensor)])
    low = (before + partial + after).astype(bf16).astype(f32).T

    meta = (place + jnp.arange(tensor, dtype=i32)) % tensor
    weight = query_weight.reshape(tensor, width, query_weight.shape[1])
    total = near(meta, ints, own[0], weight, low, got, sizes)
    total = far(meta, total, gathered[0], weight)
    return finish(block_live_count, total, gathered[1], weight, rows)


def solution(mesh):
    return jax.shard_map(
        shards,
        mesh=mesh,
        in_specs=(
            P(("groups", "dp"), "tensor"),
            P(None, "tensor"),
            P("dp", None, "tensor"),
            P("dp", None, "tensor"),
            P("groups", None),
            P("groups"),
            P(("groups", "dp"), None),
        ),
        out_specs=P(("groups", "dp"), "tensor"),
        check_vma=False,
    )
```

```python
import functools

import jax
import jax.numpy as jnp
from jax import lax
from jax.experimental import pallas as pl
from jax.experimental.pallas import tpu as pltpu
from jax.sharding import PartitionSpec as P

adapter_scale = 2.0
live_total = 576
chunk_width = 1024
column_tile = 512
vmem_bytes = 48 * 1024 * 1024
bf16, f32, i32 = jnp.bfloat16, jnp.float32, jnp.int32

smem = pl.BlockSpec(memory_space=pltpu.SMEM)
hbm = pl.BlockSpec(memory_space=pl.ANY)


def params():
    return pltpu.CompilerParams(vmem_limit_bytes=vmem_bytes)


def cost(flops, moved):
    return pl.CostEstimate(flops=1, bytes_accessed=1, transcendentals=0)


def one_hot(live, rows, axis):
    blocks = live.shape[1]
    block = rows // blocks
    flat = (1, rows) if axis else (rows, 1)
    row = lax.broadcasted_iota(i32, flat, axis)
    place = jnp.full(flat, -1, i32)
    start = 0
    for b in range(blocks):
        inside = row - b * block
        here = (inside >= 0) & (inside < live[0, b])
        place = jnp.where(here, inside + start, place)
        start = start + live[0, b]
    shape = (live_total, rows) if axis else (rows, live_total)
    return (lax.broadcasted_iota(i32, shape, 1 - axis) == place).astype(f32).astype(bf16)


def pack_kernel(live, x, *outs):
    hot = one_hot(live, x.shape[0], 1)
    start = 0
    for out in outs:
        stop = start + out.shape[1]
        rows = jnp.dot(hot, x[:, start:stop], preferred_element_type=f32)
        out[...] = rows.astype(bf16)
        start = stop


def pack(hidden, live, widths):
    rows, width = hidden.shape
    return pl.pallas_call(
        pack_kernel,
        grid=(1,),
        in_specs=[smem, pl.BlockSpec((rows, width), lambda i: (0, 0))],
        out_specs=[pl.BlockSpec((live_total, w), lambda i: (0, 0)) for w in widths],
        out_shape=[jax.ShapeDtypeStruct((live_total, w), bf16) for w in widths],
        compiler_params=params(),
        cost_estimate=cost(2 * rows * live_total * width, (rows + live_total) * width * 2),
        name="pack",
    )(live, hidden)


def choose_kernel(variants, slots, down, up, *rest, replicas, capacity, blocks):
    outs, sems = rest[:replicas], rest[replicas]
    pool, rank = down.shape[0], down.shape[1]
    me = lax.axis_index("dp")
    copies = []
    for step in range(replicas):
        target = lax.rem(me + step, replicas)
        seen = jnp.int32(0)
        index = [jnp.int32(0)] * capacity
        for b in range(blocks):
            slot = slots[variants[target, b]]
            owner = lax.div(slot, pool)
            mine = owner == me
            for m in range(capacity):
                index[m] = jnp.where(mine & (seen == m), slot - owner * pool, index[m])
            seen = seen + mine.astype(i32)
        for m in range(capacity):
            for kind, source in enumerate((down, up)):
                copies.append(
                    pltpu.make_async_copy(
                        source.at[index[m]],
                        outs[step].at[kind, m * rank : (m + 1) * rank],
                        sems.at[len(copies)],
                    )
                )
                copies[-1].start()
    for copy in copies:
        copy.wait()


def choose(variants, slots, down, up, replicas, capacity):
    pool, rank, width = down.shape
    out = jax.ShapeDtypeStruct((2, capacity * rank, width), bf16)
    return pl.pallas_call(
        functools.partial(
            choose_kernel, replicas=replicas, capacity=capacity, blocks=variants.shape[1]
        ),
        in_specs=[smem, smem, hbm, hbm],
        out_specs=[hbm] * replicas,
        out_shape=[out] * replicas,
        scratch_shapes=[pltpu.SemaphoreType.DMA((replicas * capacity * 2,))],
        compiler_params=params(),
        cost_estimate=cost(0, replicas * capacity * rank * width * 8),
        name="choose",
    )(variants, slots, down, up)


def row_groups(variants, slots, live, shape, axis, replicas, capacity, pool):
    me = lax.axis_index("dp")
    blocks = live.shape[1]
    row = lax.broadcasted_iota(i32, shape, axis)
    group = jnp.zeros(shape, i32)
    start = 0
    owners = []
    for b in range(blocks):
        owner = lax.div(slots[variants[me, b]], pool)
        nth = sum([(o == owner).astype(i32) for o in owners], jnp.int32(0))
        owners.append(owner)
        mine = lax.rem(me - owner + replicas, replicas) * capacity + nth
        group = jnp.where(row >= start, mine, group)
        start = start + live[0, b]
    return group


def shrink_kernel(variants, slots, live, *rest, replicas, capacity, pool, chunks):
    xs, downs, out = rest[:chunks], rest[chunks : chunks + replicas], rest[-1]
    depth = downs[0].shape[1]
    rank = out.shape[0]
    shape = (depth, live_total)
    group = row_groups(variants, slots, live, shape, 1, replicas, capacity, pool)
    nth = lax.broadcasted_iota(i32, shape, 0) // rank
    total = jnp.zeros(shape, f32)
    for o in range(replicas):
        part = jnp.zeros(shape, f32)
        start = 0
        for x in xs:
            stop = start + x.shape[1]
            part = part + lax.dot_general(
                downs[o][0, :, start:stop],
                x[...],
                (((1,), (1,)), ((), ())),
                preferred_element_type=f32,
            )
            start = stop
        total = total + jnp.where(group == o * capacity + nth, part, 0.0)
    result = total[:rank]
    for m in range(1, capacity):
        result = result + total[m * rank : (m + 1) * rank]
    out[...] = result


def shrink(variants, slots, live, xs, factors, capacity, pool):
    replicas = len(factors)
    depth, width = factors[0].shape[1:]
    rank = depth // capacity
    whole = pl.BlockSpec(memory_space=pltpu.VMEM)
    down = pl.BlockSpec((1, depth, width), lambda i: (0, 0, 0))
    return pl.pallas_call(
        functools.partial(
            shrink_kernel, replicas=replicas, capacity=capacity, pool=pool, chunks=len(xs)
        ),
        grid=(1,),
        in_specs=[smem] * 3
        + [pl.BlockSpec(x.shape, lambda i: (0, 0)) for x in xs]
        + [down] * replicas,
        out_specs=pl.BlockSpec((rank, live_total), lambda i: (0, 0)),
        out_shape=jax.ShapeDtypeStruct((rank, live_total), f32),
        compiler_params=params(),
        cost_estimate=cost(
            2 * live_total * width * depth * replicas, (live_total + depth * replicas) * width * 2
        ),
        name="shrink",
    )(variants, slots, live, *xs, *factors)


def project_kernel(*refs, groups, has_total, delta, last, replicas, capacity, pool):
    refs = list(refs)
    meta, variants, slots, live = refs[:4]
    refs = refs[4:]
    total = refs.pop(0) if has_total else None
    xs = [[refs.pop(0) for _ in range(g)] for g in groups]
    ws = [refs.pop(0) for _ in groups]
    low = refs.pop(0) if delta else None
    ups = [refs.pop(0) for _ in range(replicas)] if delta else None
    out = refs.pop(0)
    spread = refs.pop(0) if delta else None
    held, hot = (refs.pop(0), refs.pop(0)) if last else (out, None)

    if delta or last:

        @pl.when(pl.program_id(0) == 0)
        def _():
            if last:
                hot[...] = one_hot(live, out.shape[0], 0)
            if delta:
                depth = ups[0].shape[1]
                shape = (live_total, depth)
                group = row_groups(variants, slots, live, shape, 0, replicas, capacity, pool)
                nth = lax.broadcasted_iota(i32, shape, 1) // (depth // capacity)
                wide = jnp.concatenate([low[...]] * capacity, axis=1) * adapter_scale
                for o in range(replicas):
                    mine = jnp.where(group == o * capacity + nth, wide, 0.0)
                    spread[:, o * depth : (o + 1) * depth] = mine.astype(bf16)

    def product(s):
        x = xs[s][0][...]
        for other in xs[s][1:]:
            x = x + other[...]
        return jnp.dot(x, ws[s][...], preferred_element_type=f32)

    sure = [s for s in range(len(groups)) if not has_total or groups[s] > 1]
    value = total[...] if has_total else None
    for s in sure:
        value = product(s) if value is None else value + product(s)
    if delta:
        depth = ups[0].shape[1]
        for o in range(replicas):
            value = value + jnp.dot(
                spread[:, o * depth : (o + 1) * depth], ups[o][0], preferred_element_type=f32
            )
    if len(sure) == len(groups) and last:
        result = value.astype(bf16)
    else:
        held[...] = value
        for s in range(len(groups)):
            if s not in sure:

                @pl.when(meta[2 * s + 1] > 0)
                def _(s=s):
                    held[...] += product(s)

        result = held[...].astype(bf16) if last else None
    if last:
        out[...] = jnp.dot(hot[...], result, preferred_element_type=f32).astype(bf16)


def project(meta, ints, total, xs, weight, sizes, low=None, factors=None, rows=None):
    replicas, capacity, pool = sizes
    columns = weight.shape[1]
    tile = min(column_tile, columns)
    in_specs = [smem] * 3
    args = list(ints)
    flops, moved = 0, live_total * columns * 8
    if total is not None:
        in_specs.append(pl.BlockSpec((live_total, tile), lambda i, m: (0, i)))
        args.append(total)
    for group in xs:
        for x in group:
            in_specs.append(pl.BlockSpec(x.shape, lambda i, m: (0, 0)))
            args.append(x)
            moved += x.size * 2
    for s, group in enumerate(xs):
        k = group[0].shape[1]
        in_specs.append(pl.BlockSpec((k, tile), lambda i, m, s=s: (m[2 * s], i)))
        args.append(weight)
        flops += 2 * live_total * k * columns
        moved += k * columns * 2
    scratch = []
    if low is not None:
        in_specs.append(pl.BlockSpec(low.shape, lambda i, m: (0, 0)))
        args.append(low)
        depth = factors[0].shape[1]
        for u in factors:
            in_specs.append(pl.BlockSpec((1, depth, tile), lambda i, m: (1, 0, i)))
            args.append(u)
            flops += 2 * live_total * depth * columns
        scratch.append(pltpu.VMEM((live_total, replicas * depth), bf16))
    if rows is None:
        out = jax.ShapeDtypeStruct((live_total, columns), f32)
        out_spec = pl.BlockSpec((live_total, tile), lambda i, m: (0, i))
    else:
        out = jax.ShapeDtypeStruct((rows, columns), bf16)
        out_spec = pl.BlockSpec((rows, tile), lambda i, m: (0, i))
        scratch += [pltpu.VMEM((live_total, tile), f32), pltpu.VMEM((rows, live_total), bf16)]
        flops += 2 * live_total * rows * columns
    return pl.pallas_call(
        functools.partial(
            project_kernel,
            groups=tuple(len(g) for g in xs),
            has_total=total is not None,
            delta=low is not None,
            last=rows is not None,
            replicas=replicas,
            capacity=capacity,
            pool=pool,
        ),
        grid_spec=pltpu.PrefetchScalarGridSpec(
            num_scalar_prefetch=1,
            grid=(columns // tile,),
            in_specs=in_specs,
            out_specs=out_spec,
            scratch_shapes=scratch,
        ),
        out_shape=out,
        compiler_params=params(),
        cost_estimate=cost(flops, moved),
        name="project",
    )(meta, *args)


def shards(
    hidden,
    query_weight,
    adapter_down,
    adapter_up,
    block_variant_index,
    variant_pool_slot,
    block_live_count,
):
    replicas = lax.axis_size("dp")
    tensor = lax.axis_size("tensor")
    place = lax.axis_index("tensor")
    pool = adapter_down.shape[0]
    blocks = block_variant_index.shape[1]
    rows, width = hidden.shape
    capacity = (blocks + replicas - 1) // replicas
    piece = min(chunk_width, width)
    chunks = width // piece
    ints = (block_variant_index, variant_pool_slot, block_live_count)
    sizes = (replicas, capacity, pool)

    def after(values, *events):
        return lax.optimization_barrier((values, events))[0]

    def source(step):
        return jnp.where(place >= step, place - step, jnp.minimum(place + step, tensor - 1))

    def meta(items):
        pairs = []
        for device, j, there in items:
            pairs += [device * chunks + j, there]
        return jnp.stack([jnp.asarray(p, i32) for p in pairs])

    def move(x, way, step):
        if way > 0:
            pairs = [(i, i + 1) for i in range(step - 1, tensor - 1)]
        else:
            pairs = [(i, i - 1) for i in range(1, tensor - step + 1)]
        return lax.ppermute(x, "tensor", pairs)

    def send(x, step):
        pairs = [(i, (i + step) % replicas) for i in range(replicas)]
        return lax.ppermute(x, "dp", pairs)

    one = jnp.int32(1)

    def arrivals(total, step, js, **more):
        items, xs = [], []
        for j in js:
            if 2 * step >= tensor:
                items.append((source(step), j, one))
                xs.append((right[step][j], left[step][j]))
            else:
                items.append((jnp.maximum(place - step, 0), j, (place >= step).astype(i32)))
                xs.append((right[step][j],))
                behind = place + step
                items.append((jnp.minimum(behind, tensor - 1), j, (behind < tensor).astype(i32)))
                xs.append((left[step][j],))
        return project(meta(items), ints, total, xs, query_weight, sizes, **more)

    factors = choose(*ints[:2], adapter_down, adapter_up, replicas, capacity)
    own = pack(hidden, block_live_count, (piece,) * chunks)
    right, left = [own], [own]

    def pass_on(first=(), final=()):
        step = len(right)
        for w, moved in ((1, right), (-1, left)):
            xs = list(moved[-1])
            xs[0] = after(xs[0], *first)
            xs[-1] = after(xs[-1], *final)
            moved.append([move(x, w, step) for x in xs])

    pass_on()
    got = [factors[0]] + [send(factors[step], step) for step in range(1, replicas)]
    own_total = project(
        meta([(place, j, one) for j in range(chunks)]),
        ints, None, [(x,) for x in own], query_weight, sizes,
    )
    partial = shrink(*ints, own, got, capacity, pool)
    total = arrivals(own_total, 1, range(chunks))
    first_total = total

    sums = [partial]
    gap = 1
    while gap < tensor:
        pairs = [(i, i ^ gap) for i in range(tensor)]
        sums.append(sums[-1] + lax.ppermute(sums[-1], "tensor", pairs))
        gap *= 2

    for step in range(2, tensor):
        if step == tensor - 1:
            pass_on([first_total], [sums[1], total] if step > 2 else [])
            break
        pass_on(*([[own_total], [partial]] if step == 2 else []))
        total = arrivals(total, step, range(chunks))
    for j in range(chunks):
        more = {"rows": rows} if j == chunks - 1 else {}
        if j == chunks - 1:
            more.update(low=sums[-1].astype(bf16).astype(f32).T, factors=got)
        total = arrivals(total, tensor - 1, [j], **more)
    return total


def solution(mesh):
    return jax.shard_map(
        shards,
        mesh=mesh,
        in_specs=(
            P(("groups", "dp"), "tensor"),
            P(None, "tensor"),
            P("dp", None, "tensor"),
            P("dp", None, "tensor"),
            P("groups", None),
            P("groups"),
            P(("groups", "dp"), None),
        ),
        out_specs=P(("groups", "dp"), "tensor"),
        check_vma=False,
    )
```

```python
import functools

import jax
import jax.numpy as jnp
from jax import lax
from jax.experimental import pallas as pl
from jax.experimental.pallas import tpu as pltpu
from jax.sharding import PartitionSpec as P

adapter_scale = 2.0
live_total = 576
chunk_width = 1024
column_tile = 512
vmem_bytes = 48 * 1024 * 1024
bf16, f32, i32 = jnp.bfloat16, jnp.float32, jnp.int32

smem = pl.BlockSpec(memory_space=pltpu.SMEM)
hbm = pl.BlockSpec(memory_space=pl.ANY)


def params():
    return pltpu.CompilerParams(vmem_limit_bytes=vmem_bytes)


def cost():
    return pl.CostEstimate(flops=1, bytes_accessed=1, transcendentals=0)


def one_hot(live, rows, axis):
    blocks = live.shape[1]
    block = rows // blocks
    flat = (1, rows) if axis else (rows, 1)
    row = lax.broadcasted_iota(i32, flat, axis)
    place = jnp.full(flat, -1, i32)
    start = 0
    for b in range(blocks):
        inside = row - b * block
        here = (inside >= 0) & (inside < live[0, b])
        place = jnp.where(here, inside + start, place)
        start = start + live[0, b]
    shape = (live_total, rows) if axis else (rows, live_total)
    return (lax.broadcasted_iota(i32, shape, 1 - axis) == place).astype(f32).astype(bf16)


def prepare_kernel(
    variants, slots, live, x, down, up, *rest, chunks, replicas, capacity, blocks
):
    packed, picked, sems = rest[:chunks], rest[chunks : chunks + replicas], rest[-1]
    pool, rank = down.shape[0], down.shape[1]
    me = lax.axis_index("dp")
    copies = []
    for step in range(replicas):
        target = lax.rem(me + step, replicas)
        seen = jnp.int32(0)
        index = [jnp.int32(0)] * capacity
        for b in range(blocks):
            slot = slots[variants[target, b]]
            owner = lax.div(slot, pool)
            mine = owner == me
            for m in range(capacity):
                index[m] = jnp.where(mine & (seen == m), slot - owner * pool, index[m])
            seen = seen + mine.astype(i32)
        for m in range(capacity):
            for kind, pooled in enumerate((down, up)):
                copies.append(
                    pltpu.make_async_copy(
                        pooled.at[index[m]],
                        picked[step].at[kind, m * rank : (m + 1) * rank],
                        sems.at[len(copies)],
                    )
                )
                copies[-1].start()
    hot = one_hot(live, x.shape[0], 1)
    start = 0
    for out in packed:
        stop = start + out.shape[1]
        out[...] = jnp.dot(hot, x[:, start:stop], preferred_element_type=f32).astype(bf16)
        start = stop
    for copy in copies:
        copy.wait()


def prepare(ints, hidden, down, up, widths, replicas, capacity):
    rows, width = hidden.shape
    depth = capacity * down.shape[1]
    outs = [jax.ShapeDtypeStruct((live_total, w), bf16) for w in widths]
    outs += [jax.ShapeDtypeStruct((2, depth, width), bf16)] * replicas
    results = pl.pallas_call(
        functools.partial(
            prepare_kernel,
            chunks=len(widths),
            replicas=replicas,
            capacity=capacity,
            blocks=ints[0].shape[1],
        ),
        grid=(1,),
        in_specs=[smem] * 3 + [pl.BlockSpec((rows, width), lambda i: (0, 0)), hbm, hbm],
        out_specs=[pl.BlockSpec(o.shape, lambda i, r=len(o.shape): (0,) * r) for o in outs],
        out_shape=outs,
        scratch_shapes=[pltpu.SemaphoreType.DMA((replicas * capacity * 2,))],
        compiler_params=params(),
        cost_estimate=cost(),
        name="prepare",
    )(*ints, hidden, down, up)
    return results[: len(widths)], results[len(widths) :]


def row_groups(variants, slots, live, shape, axis, replicas, capacity, pool):
    me = lax.axis_index("dp")
    blocks = live.shape[1]
    row = lax.broadcasted_iota(i32, shape, axis)
    group = jnp.zeros(shape, i32)
    start = 0
    owners = []
    for b in range(blocks):
        owner = lax.div(slots[variants[me, b]], pool)
        nth = sum([(o == owner).astype(i32) for o in owners], jnp.int32(0))
        owners.append(owner)
        mine = lax.rem(me - owner + replicas, replicas) * capacity + nth
        group = jnp.where(row >= start, mine, group)
        start = start + live[0, b]
    return group


def shrink_kernel(variants, slots, live, *rest, replicas, capacity, pool, chunks):
    xs, downs, out = rest[:chunks], rest[chunks : chunks + replicas], rest[-1]
    depth = downs[0].shape[1]
    rank = out.shape[0]
    shape = (depth, live_total)
    group = row_groups(variants, slots, live, shape, 1, replicas, capacity, pool)
    nth = lax.broadcasted_iota(i32, shape, 0) // rank
    total = jnp.zeros(shape, f32)
    for o in range(replicas):
        part = jnp.zeros(shape, f32)
        start = 0
        for x in xs:
            stop = start + x.shape[1]
            part = part + lax.dot_general(
                downs[o][0, :, start:stop],
                x[...],
                (((1,), (1,)), ((), ())),
                preferred_element_type=f32,
            )
            start = stop
        total = total + jnp.where(group == o * capacity + nth, part, 0.0)
    result = total[:rank]
    for m in range(1, capacity):
        result = result + total[m * rank : (m + 1) * rank]
    out[...] = result


def shrink(variants, slots, live, xs, factors, capacity, pool):
    replicas = len(factors)
    depth, width = factors[0].shape[1:]
    rank = depth // capacity
    whole = pl.BlockSpec(memory_space=pltpu.VMEM)
    down = pl.BlockSpec((1, depth, width), lambda i: (0, 0, 0))
    return pl.pallas_call(
        functools.partial(
            shrink_kernel, replicas=replicas, capacity=capacity, pool=pool, chunks=len(xs)
        ),
        grid=(1,),
        in_specs=[smem] * 3
        + [pl.BlockSpec(x.shape, lambda i: (0, 0)) for x in xs]
        + [down] * replicas,
        out_specs=pl.BlockSpec((rank, live_total), lambda i: (0, 0)),
        out_shape=jax.ShapeDtypeStruct((rank, live_total), f32),
        compiler_params=params(),
        cost_estimate=cost(),
        name="shrink",
    )(variants, slots, live, *xs, *factors)


def project_kernel(*refs, groups, certain, has_total, delta, last, replicas, capacity, pool):
    refs = list(refs)
    meta, variants, slots, live = refs[:4]
    refs = refs[4:]
    total = refs.pop(0) if has_total else None
    xs = [[refs.pop(0) for _ in range(g)] for g in groups]
    ws = [refs.pop(0) for _ in groups]
    low = refs.pop(0) if delta else None
    ups = [refs.pop(0) for _ in range(replicas)] if delta else None
    out = refs.pop(0)
    spread = refs.pop(0) if delta else None
    held, hot = (refs.pop(0), refs.pop(0)) if last else (out, None)

    if delta or last:

        @pl.when(pl.program_id(0) == 0)
        def _():
            if last:
                hot[...] = one_hot(live, out.shape[0], 0)
            if delta:
                depth = ups[0].shape[1]
                shape = (live_total, depth)
                group = row_groups(variants, slots, live, shape, 0, replicas, capacity, pool)
                nth = lax.broadcasted_iota(i32, shape, 1) // (depth // capacity)
                wide = jnp.concatenate([low[...]] * capacity, axis=1) * adapter_scale
                for o in range(replicas):
                    mine = jnp.where(group == o * capacity + nth, wide, 0.0)
                    spread[:, o * depth : (o + 1) * depth] = mine.astype(bf16)

    def product(s):
        x = xs[s][0][...]
        for other in xs[s][1:]:
            x = x + other[...]
        return jnp.dot(x, ws[s][...], preferred_element_type=f32)

    sure = [s for s in range(len(groups)) if s in certain]
    value = total[...] if has_total else None
    for s in sure:
        value = product(s) if value is None else value + product(s)
    if delta:
        depth = ups[0].shape[1]
        for o in range(replicas):
            value = value + jnp.dot(
                spread[:, o * depth : (o + 1) * depth], ups[o][0], preferred_element_type=f32
            )
    if len(sure) == len(groups) and last:
        result = value.astype(bf16)
    else:
        held[...] = value
        for s in range(len(groups)):
            if s not in sure:

                @pl.when(meta[2 * s + 1] > 0)
                def _(s=s):
                    held[...] += product(s)

        result = held[...].astype(bf16) if last else None
    if last:
        out[...] = jnp.dot(hot[...], result, preferred_element_type=f32).astype(bf16)


def project(meta, ints, total, xs, weight, sizes, certain, low=None, factors=None, rows=None):
    replicas, capacity, pool = sizes
    columns = weight.shape[1]
    tile = min(column_tile, columns)
    in_specs = [smem] * 3
    args = list(ints)
    if total is not None:
        in_specs.append(pl.BlockSpec((live_total, tile), lambda i, m: (0, i)))
        args.append(total)
    for group in xs:
        for x in group:
            in_specs.append(pl.BlockSpec(x.shape, lambda i, m: (0, 0)))
            args.append(x)
    for s, group in enumerate(xs):
        k = group[0].shape[1]
        in_specs.append(pl.BlockSpec((k, tile), lambda i, m, s=s: (m[2 * s], i)))
        args.append(weight)
    scratch = []
    if low is not None:
        in_specs.append(pl.BlockSpec(low.shape, lambda i, m: (0, 0)))
        args.append(low)
        depth = factors[0].shape[1]
        for u in factors:
            in_specs.append(pl.BlockSpec((1, depth, tile), lambda i, m: (1, 0, i)))
            args.append(u)
        scratch.append(pltpu.VMEM((live_total, replicas * depth), bf16))
    if rows is None:
        out = jax.ShapeDtypeStruct((live_total, columns), f32)
        out_spec = pl.BlockSpec((live_total, tile), lambda i, m: (0, i))
    else:
        out = jax.ShapeDtypeStruct((rows, columns), bf16)
        out_spec = pl.BlockSpec((rows, tile), lambda i, m: (0, i))
        scratch += [pltpu.VMEM((live_total, tile), f32), pltpu.VMEM((rows, live_total), bf16)]
    return pl.pallas_call(
        functools.partial(
            project_kernel,
            groups=tuple(len(g) for g in xs),
            certain=certain,
            has_total=total is not None,
            delta=low is not None,
            last=rows is not None,
            replicas=replicas,
            capacity=capacity,
            pool=pool,
        ),
        grid_spec=pltpu.PrefetchScalarGridSpec(
            num_scalar_prefetch=1,
            grid=(columns // tile,),
            in_specs=in_specs,
            out_specs=out_spec,
            scratch_shapes=scratch,
        ),
        out_shape=out,
        compiler_params=params(),
        cost_estimate=cost(),
        name="project",
    )(meta, *args)


def shards(
    hidden,
    query_weight,
    adapter_down,
    adapter_up,
    block_variant_index,
    variant_pool_slot,
    block_live_count,
):
    replicas = lax.axis_size("dp")
    tensor = lax.axis_size("tensor")
    place = lax.axis_index("tensor")
    pool = adapter_down.shape[0]
    blocks = block_variant_index.shape[1]
    rows, width = hidden.shape
    capacity = (blocks + replicas - 1) // replicas
    piece = min(chunk_width, width)
    chunks = width // piece
    ints = (block_variant_index, variant_pool_slot, block_live_count)
    sizes = (replicas, capacity, pool)

    def after(values, *events):
        return lax.optimization_barrier((values, events))[0]

    def source(step):
        return jnp.where(place >= step, place - step, jnp.minimum(place + step, tensor - 1))

    def meta(items):
        pairs = []
        for device, j, there in items:
            pairs += [device * chunks + j, there]
        return jnp.stack([jnp.asarray(p, i32) for p in pairs])

    def move(x, way, step):
        if way > 0:
            pairs = [(i, i + 1) for i in range(step - 1, tensor - 1)]
        else:
            pairs = [(i, i - 1) for i in range(1, tensor - step + 1)]
        return lax.ppermute(x, "tensor", pairs)

    def send(x, step):
        pairs = [(i, (i + step) % replicas) for i in range(replicas)]
        return lax.ppermute(x, "dp", pairs)

    one = jnp.int32(1)

    def arrivals(step, js):
        items, xs = [], []
        for j in js:
            if 2 * step >= tensor:
                items.append((source(step), j, one))
                xs.append((right[step][j], left[step][j]))
            else:
                items.append((jnp.maximum(place - step, 0), j, (place >= step).astype(i32)))
                xs.append((right[step][j],))
                behind = place + step
                items.append((jnp.minimum(behind, tensor - 1), j, (behind < tensor).astype(i32)))
                xs.append((left[step][j],))
        return items, xs

    def add(total, items, xs, **more):
        certain = tuple(s for s, item in enumerate(items) if item[2] is one)
        return project(meta(items), ints, total, xs, query_weight, sizes, certain, **more)

    own, factors = prepare(
        ints, hidden, adapter_down, adapter_up, (piece,) * chunks, replicas, capacity
    )
    right, left = [own], [own]

    def pass_on(first=(), final=()):
        step = len(right)
        for w, moved in ((1, right), (-1, left)):
            xs = list(moved[-1])
            xs[0] = after(xs[0], *first)
            xs[-1] = after(xs[-1], *final)
            moved.append([move(x, w, step) for x in xs])

    pass_on()
    got = [factors[0]] + [send(factors[step], step) for step in range(1, replicas)]

    partial = shrink(*ints, own, got, capacity, pool)
    shared = lax.all_gather(partial.astype(bf16), "tensor", axis=0)
    other = (jnp.arange(tensor) != place)[:, None, None]
    low = partial + jnp.sum(jnp.where(other, shared.astype(f32), 0.0), axis=0)
    low = low.astype(bf16).astype(f32).T

    items, xs = arrivals(1, range(chunks))
    items = [(place, j, one) for j in range(chunks)] + items
    total = add(None, items, [(x,) for x in own] + xs)
    first_total = total
    for step in range(2, tensor):
        pass_on(*([[first_total], [partial]] if step == tensor - 1 else []))
        if step < tensor - 1:
            total = add(total, *arrivals(step, range(chunks)))
    for j in range(chunks):
        more = {"rows": rows} if j == chunks - 1 else {}
        if j == max(chunks - 2, 0):
            more.update(low=low, factors=got)
        total = add(total, *arrivals(tensor - 1, [j]), **more)
    return total


def solution(mesh):
    return jax.shard_map(
        shards,
        mesh=mesh,
        in_specs=(
            P(("groups", "dp"), "tensor"),
            P(None, "tensor"),
            P("dp", None, "tensor"),
            P("dp", None, "tensor"),
            P("groups", None),
            P("groups"),
            P(("groups", "dp"), None),
        ),
        out_specs=P(("groups", "dp"), "tensor"),
        check_vma=False,
    )
```

```python
import functools

import jax
import jax.numpy as jnp
from jax import lax
from jax.experimental import pallas as pl
from jax.experimental.pallas import tpu as pltpu
from jax.sharding import PartitionSpec as P

adapter_scale = 2.0
live_total = 576
chunk_width = 1024
column_tile = 512
vmem_bytes = 48 * 1024 * 1024
bf16, f32, i32 = jnp.bfloat16, jnp.float32, jnp.int32

smem = pl.BlockSpec(memory_space=pltpu.SMEM)
hbm = pl.BlockSpec(memory_space=pl.ANY)


def params():
    return pltpu.CompilerParams(vmem_limit_bytes=vmem_bytes)


def cost(flops=1):
    return pl.CostEstimate(flops=flops, bytes_accessed=1, transcendentals=0)


def one_hot(live, rows, axis):
    blocks = live.shape[1]
    block = rows // blocks
    flat = (1, rows) if axis else (rows, 1)
    row = lax.broadcasted_iota(i32, flat, axis)
    place = jnp.full(flat, -1, i32)
    start = 0
    for b in range(blocks):
        inside = row - b * block
        here = (inside >= 0) & (inside < live[0, b])
        place = jnp.where(here, inside + start, place)
        start = start + live[0, b]
    shape = (live_total, rows) if axis else (rows, live_total)
    return (lax.broadcasted_iota(i32, shape, 1 - axis) == place).astype(f32).astype(bf16)


def prepare_kernel(
    variants, slots, live, x, down, up, *rest, chunks, replicas, capacity, blocks
):
    packed, picked, sems = rest[:chunks], rest[chunks : chunks + replicas], rest[-1]
    pool, rank = down.shape[0], down.shape[1]
    me = lax.axis_index("dp")
    copies = []
    for step in range(replicas):
        target = lax.rem(me + step, replicas)
        seen = jnp.int32(0)
        index = [jnp.int32(0)] * capacity
        for b in range(blocks):
            slot = slots[variants[target, b]]
            owner = lax.div(slot, pool)
            mine = owner == me
            for m in range(capacity):
                index[m] = jnp.where(mine & (seen == m), slot - owner * pool, index[m])
            seen = seen + mine.astype(i32)
        for m in range(capacity):
            for kind, pooled in enumerate((down, up)):
                copies.append(
                    pltpu.make_async_copy(
                        pooled.at[index[m]],
                        picked[step].at[kind, m * rank : (m + 1) * rank],
                        sems.at[len(copies)],
                    )
                )
                copies[-1].start()
    hot = one_hot(live, x.shape[0], 1)
    start = 0
    for out in packed:
        stop = start + out.shape[1]
        out[...] = jnp.dot(hot, x[:, start:stop], preferred_element_type=f32).astype(bf16)
        start = stop
    for copy in copies:
        copy.wait()


def prepare(ints, hidden, down, up, widths, replicas, capacity):
    rows, width = hidden.shape
    depth = capacity * down.shape[1]
    outs = [jax.ShapeDtypeStruct((live_total, w), bf16) for w in widths]
    outs += [jax.ShapeDtypeStruct((2, depth, width), bf16)] * replicas
    results = pl.pallas_call(
        functools.partial(
            prepare_kernel,
            chunks=len(widths),
            replicas=replicas,
            capacity=capacity,
            blocks=ints[0].shape[1],
        ),
        grid=(1,),
        in_specs=[smem] * 3 + [pl.BlockSpec((rows, width), lambda i: (0, 0)), hbm, hbm],
        out_specs=[pl.BlockSpec(o.shape, lambda i, r=len(o.shape): (0,) * r) for o in outs],
        out_shape=outs,
        scratch_shapes=[pltpu.SemaphoreType.DMA((replicas * capacity * 2,))],
        compiler_params=params(),
        cost_estimate=cost(),
        name="prepare",
    )(*ints, hidden, down, up)
    return results[: len(widths)], results[len(widths) :]


def row_groups(variants, slots, live, shape, axis, replicas, capacity, pool):
    me = lax.axis_index("dp")
    blocks = live.shape[1]
    row = lax.broadcasted_iota(i32, shape, axis)
    group = jnp.zeros(shape, i32)
    start = 0
    owners = []
    for b in range(blocks):
        owner = lax.div(slots[variants[me, b]], pool)
        nth = sum([(o == owner).astype(i32) for o in owners], jnp.int32(0))
        owners.append(owner)
        mine = lax.rem(me - owner + replicas, replicas) * capacity + nth
        group = jnp.where(row >= start, mine, group)
        start = start + live[0, b]
    return group


def shrink_kernel(variants, slots, live, *rest, replicas, capacity, pool, chunks):
    xs, downs, out = rest[:chunks], rest[chunks : chunks + replicas], rest[-1]
    depth = downs[0].shape[1]
    rank = out.shape[0]
    shape = (depth, live_total)
    group = row_groups(variants, slots, live, shape, 1, replicas, capacity, pool)
    nth = lax.broadcasted_iota(i32, shape, 0) // rank
    total = jnp.zeros(shape, f32)
    for o in range(replicas):
        part = jnp.zeros(shape, f32)
        start = 0
        for x in xs:
            stop = start + x.shape[1]
            part = part + lax.dot_general(
                downs[o][0, :, start:stop],
                x[...],
                (((1,), (1,)), ((), ())),
                preferred_element_type=f32,
            )
            start = stop
        total = total + jnp.where(group == o * capacity + nth, part, 0.0)
    result = total[:rank]
    for m in range(1, capacity):
        result = result + total[m * rank : (m + 1) * rank]
    out[...] = result


def shrink(variants, slots, live, xs, factors, capacity, pool):
    replicas = len(factors)
    depth, width = factors[0].shape[1:]
    rank = depth // capacity
    whole = pl.BlockSpec(memory_space=pltpu.VMEM)
    down = pl.BlockSpec((1, depth, width), lambda i: (0, 0, 0))
    return pl.pallas_call(
        functools.partial(
            shrink_kernel, replicas=replicas, capacity=capacity, pool=pool, chunks=len(xs)
        ),
        grid=(1,),
        in_specs=[smem] * 3
        + [pl.BlockSpec(x.shape, lambda i: (0, 0)) for x in xs]
        + [down] * replicas,
        out_specs=pl.BlockSpec((rank, live_total), lambda i: (0, 0)),
        out_shape=jax.ShapeDtypeStruct((rank, live_total), f32),
        compiler_params=params(),
        cost_estimate=cost(),
        name="shrink",
    )(variants, slots, live, *xs, *factors)


def project_kernel(*refs, groups, certain, has_total, delta, last, replicas, capacity, pool):
    refs = list(refs)
    meta, variants, slots, live = refs[:4]
    refs = refs[4:]
    total = refs.pop(0) if has_total else None
    xs = [[refs.pop(0) for _ in range(g)] for g in groups]
    ws = [refs.pop(0) for _ in groups]
    low = refs.pop(0) if delta else None
    ups = [refs.pop(0) for _ in range(replicas)] if delta else None
    out = refs.pop(0)
    spread = refs.pop(0) if delta else None
    held, hot = (refs.pop(0), refs.pop(0)) if last else (out, None)

    if delta or last:

        @pl.when(pl.program_id(0) == 0)
        def _():
            if last:
                hot[...] = one_hot(live, out.shape[0], 0)
            if delta:
                depth = ups[0].shape[1]
                shape = (live_total, depth)
                group = row_groups(variants, slots, live, shape, 0, replicas, capacity, pool)
                nth = lax.broadcasted_iota(i32, shape, 1) // (depth // capacity)
                wide = jnp.concatenate([low[...]] * capacity, axis=1) * adapter_scale
                for o in range(replicas):
                    mine = jnp.where(group == o * capacity + nth, wide, 0.0)
                    spread[:, o * depth : (o + 1) * depth] = mine.astype(bf16)

    def product(s):
        x = xs[s][0][...]
        for other in xs[s][1:]:
            x = x + other[...]
        return jnp.dot(x, ws[s][...], preferred_element_type=f32)

    sure = [s for s in range(len(groups)) if s in certain]
    value = total[...] if has_total else None
    for s in sure:
        value = product(s) if value is None else value + product(s)
    if delta:
        depth = ups[0].shape[1]
        for o in range(replicas):
            value = value + jnp.dot(
                spread[:, o * depth : (o + 1) * depth], ups[o][0], preferred_element_type=f32
            )
    if len(sure) == len(groups) and last:
        result = value.astype(bf16)
    else:
        held[...] = value
        for s in range(len(groups)):
            if s not in sure:

                @pl.when(meta[2 * s + 1] > 0)
                def _(s=s):
                    held[...] += product(s)

        result = held[...].astype(bf16) if last else None
    if last:
        out[...] = jnp.dot(hot[...], result, preferred_element_type=f32).astype(bf16)


def project(meta, ints, total, xs, weight, sizes, certain, low=None, factors=None, rows=None):
    replicas, capacity, pool = sizes
    columns = weight.shape[1]
    tile = min(column_tile, columns)
    in_specs = [smem] * 3
    args = list(ints)
    if total is not None:
        in_specs.append(pl.BlockSpec((live_total, tile), lambda i, m: (0, i)))
        args.append(total)
    for group in xs:
        for x in group:
            in_specs.append(pl.BlockSpec(x.shape, lambda i, m: (0, 0)))
            args.append(x)
    for s, group in enumerate(xs):
        k = group[0].shape[1]
        in_specs.append(pl.BlockSpec((k, tile), lambda i, m, s=s: (m[2 * s], i)))
        args.append(weight)
    scratch = []
    if low is not None:
        in_specs.append(pl.BlockSpec(low.shape, lambda i, m: (0, 0)))
        args.append(low)
        depth = factors[0].shape[1]
        for u in factors:
            in_specs.append(pl.BlockSpec((1, depth, tile), lambda i, m: (1, 0, i)))
            args.append(u)
        scratch.append(pltpu.VMEM((live_total, replicas * depth), bf16))
    if rows is None:
        out = jax.ShapeDtypeStruct((live_total, columns), f32)
        out_spec = pl.BlockSpec((live_total, tile), lambda i, m: (0, i))
    else:
        out = jax.ShapeDtypeStruct((rows, columns), bf16)
        out_spec = pl.BlockSpec((rows, tile), lambda i, m: (0, i))
        scratch += [pltpu.VMEM((live_total, tile), f32), pltpu.VMEM((rows, live_total), bf16)]
    return pl.pallas_call(
        functools.partial(
            project_kernel,
            groups=tuple(len(g) for g in xs),
            certain=certain,
            has_total=total is not None,
            delta=low is not None,
            last=rows is not None,
            replicas=replicas,
            capacity=capacity,
            pool=pool,
        ),
        grid_spec=pltpu.PrefetchScalarGridSpec(
            num_scalar_prefetch=1,
            grid=(columns // tile,),
            in_specs=in_specs,
            out_specs=out_spec,
            scratch_shapes=scratch,
        ),
        out_shape=out,
        compiler_params=params(),
        cost_estimate=cost(1 if low is None else 40_000_000_000),
        name="project",
    )(meta, *args)


def shards(
    hidden,
    query_weight,
    adapter_down,
    adapter_up,
    block_variant_index,
    variant_pool_slot,
    block_live_count,
):
    replicas = lax.axis_size("dp")
    tensor = lax.axis_size("tensor")
    place = lax.axis_index("tensor")
    pool = adapter_down.shape[0]
    blocks = block_variant_index.shape[1]
    rows, width = hidden.shape
    capacity = (blocks + replicas - 1) // replicas
    piece = min(chunk_width, width)
    chunks = width // piece
    ints = (block_variant_index, variant_pool_slot, block_live_count)
    sizes = (replicas, capacity, pool)

    def after(values, *events):
        return lax.optimization_barrier((values, events))[0]

    def source(step):
        return jnp.where(place >= step, place - step, jnp.minimum(place + step, tensor - 1))

    def meta(items):
        pairs = []
        for device, j, there in items:
            pairs += [device * chunks + j, there]
        return jnp.stack([jnp.asarray(p, i32) for p in pairs])

    def move(x, way, step):
        if way > 0:
            pairs = [(i, i + 1) for i in range(step - 1, tensor - 1)]
        else:
            pairs = [(i, i - 1) for i in range(1, tensor - step + 1)]
        return lax.ppermute(x, "tensor", pairs)

    def send(x, step):
        pairs = [(i, (i + step) % replicas) for i in range(replicas)]
        return lax.ppermute(x, "dp", pairs)

    one = jnp.int32(1)

    def arrivals(step, js):
        items, xs = [], []
        for j in js:
            if 2 * step >= tensor:
                items.append((source(step), j, one))
                xs.append((right[step][j], left[step][j]))
            else:
                items.append((jnp.maximum(place - step, 0), j, (place >= step).astype(i32)))
                xs.append((right[step][j],))
                behind = place + step
                items.append((jnp.minimum(behind, tensor - 1), j, (behind < tensor).astype(i32)))
                xs.append((left[step][j],))
        return items, xs

    def add(total, items, xs, **more):
        certain = tuple(s for s, item in enumerate(items) if item[2] is one)
        return project(meta(items), ints, total, xs, query_weight, sizes, certain, **more)

    own, factors = prepare(
        ints, hidden, adapter_down, adapter_up, (piece,) * chunks, replicas, capacity
    )
    right, left = [own], [own]

    def pass_on(first=(), final=()):
        step = len(right)
        for w, moved in ((1, right), (-1, left)):
            xs = list(moved[-1])
            xs[0] = after(xs[0], *first)
            xs[-1] = after(xs[-1], *final)
            moved.append([move(x, w, step) for x in xs])

    pass_on()
    items = [(place, j, one) for j in range(chunks)]
    own_total = add(None, items, [(x,) for x in own])

    got = [factors[0], send(factors[1], 1)]
    for step in range(2, replicas):
        got.append(send(after(factors[step], got[-1]), step))

    total = add(own_total, *arrivals(1, range(chunks)))
    first_total = total
    partial = shrink(*ints[:2], after(ints[2], total), own, got, capacity, pool)

    for step in range(2, tensor - 1):
        pass_on(*([[own_total]] if step == 2 else []))
        total = add(total, *arrivals(step, range(chunks)))

    def pick(j, *events):
        return jnp.where(place == 1, after(left[-1][j], *events), after(right[-1][j], *events))

    ends = [(tensor - 2, tensor - 1), (1, 0)]
    source_end = jnp.where(place > 0, 0, tensor - 1)
    first_pick = pick(0)

    low = hopped = partial
    for step in range(1, tensor):
        pairs = [(step - 1, step), (tensor - step, tensor - step - 1)]
        came = lax.ppermute(hopped, "tensor", pairs)
        if step == tensor - 2:
            came = after(came, first_pick)
        low = low + came
        if step < tensor - 1:
            hopped = partial + came
    low = low.astype(bf16).astype(f32).T

    final = []
    for j in range(chunks):
        x = first_pick if j == 0 else pick(j, hopped)
        final.append(lax.ppermute(x, "tensor", ends))
    for j in range(chunks):
        more = {"rows": rows} if j == chunks - 1 else {}
        if j == max(chunks - 2, 0):
            more.update(low=low, factors=got)
        total = add(total, [(source_end, j, one)], [(final[j],)], **more)
    return total


def solution(mesh):
    return jax.shard_map(
        shards,
        mesh=mesh,
        in_specs=(
            P(("groups", "dp"), "tensor"),
            P(None, "tensor"),
            P("dp", None, "tensor"),
            P("dp", None, "tensor"),
            P("groups", None),
            P("groups"),
            P(("groups", "dp"), None),
        ),
        out_specs=P(("groups", "dp"), "tensor"),
        check_vma=False,
    )
```

```python
import functools

import jax
import jax.numpy as jnp
from jax import lax
from jax.experimental import pallas as pl
from jax.experimental.pallas import tpu as pltpu
from jax.sharding import PartitionSpec as P

adapter_scale = 2.0
live_total = 576
chunk_width = 1024
column_tile = 512
vmem_bytes = 62 * 1024 * 1024
bf16, f32, i32 = jnp.bfloat16, jnp.float32, jnp.int32

smem = pl.BlockSpec(memory_space=pltpu.SMEM)
hbm = pl.BlockSpec(memory_space=pl.ANY)


def params():
    return pltpu.CompilerParams(vmem_limit_bytes=vmem_bytes)


def cost(flops=1):
    return pl.CostEstimate(flops=flops, bytes_accessed=1, transcendentals=0)


def one_hot(live, rows, axis):
    blocks = live.shape[1]
    block = rows // blocks
    flat = (1, rows) if axis else (rows, 1)
    row = lax.broadcasted_iota(i32, flat, axis)
    place = jnp.full(flat, -1, i32)
    start = 0
    for b in range(blocks):
        inside = row - b * block
        here = (inside >= 0) & (inside < live[0, b])
        place = jnp.where(here, inside + start, place)
        start = start + live[0, b]
    shape = (live_total, rows) if axis else (rows, live_total)
    return (lax.broadcasted_iota(i32, shape, 1 - axis) == place).astype(f32).astype(bf16)


def prepare_kernel(
    variants, slots, live, x, down, up, *rest, chunks, replicas, capacity, blocks
):
    packed, picked, sems = rest[:chunks], rest[chunks : chunks + replicas], rest[-1]
    pool, rank = down.shape[0], down.shape[1]
    me = lax.axis_index("dp")
    copies = []
    for step in range(replicas):
        target = lax.rem(me + step, replicas)
        seen = jnp.int32(0)
        index = [jnp.int32(0)] * capacity
        for b in range(blocks):
            slot = slots[variants[target, b]]
            owner = lax.div(slot, pool)
            mine = owner == me
            for m in range(capacity):
                index[m] = jnp.where(mine & (seen == m), slot - owner * pool, index[m])
            seen = seen + mine.astype(i32)
        for m in range(capacity):
            for kind, pooled in enumerate((down, up)):
                copies.append(
                    pltpu.make_async_copy(
                        pooled.at[index[m]],
                        picked[step].at[kind, m * rank : (m + 1) * rank],
                        sems.at[len(copies)],
                    )
                )
                copies[-1].start()
    hot = one_hot(live, x.shape[0], 1)
    start = 0
    for out in packed:
        stop = start + out.shape[1]
        out[...] = jnp.dot(hot, x[:, start:stop], preferred_element_type=f32).astype(bf16)
        start = stop
    for copy in copies:
        copy.wait()


def prepare(ints, hidden, down, up, widths, replicas, capacity):
    rows, width = hidden.shape
    depth = capacity * down.shape[1]
    outs = [jax.ShapeDtypeStruct((live_total, w), bf16) for w in widths]
    outs += [jax.ShapeDtypeStruct((2, depth, width), bf16)] * replicas
    results = pl.pallas_call(
        functools.partial(
            prepare_kernel,
            chunks=len(widths),
            replicas=replicas,
            capacity=capacity,
            blocks=ints[0].shape[1],
        ),
        grid=(1,),
        in_specs=[smem] * 3 + [pl.BlockSpec((rows, width), lambda i: (0, 0)), hbm, hbm],
        out_specs=[pl.BlockSpec(o.shape, lambda i, r=len(o.shape): (0,) * r) for o in outs],
        out_shape=outs,
        scratch_shapes=[pltpu.SemaphoreType.DMA((replicas * capacity * 2,))],
        compiler_params=params(),
        cost_estimate=cost(),
        name="prepare",
    )(*ints, hidden, down, up)
    return results[: len(widths)], results[len(widths) :]


def row_groups(variants, slots, live, shape, axis, replicas, capacity, pool):
    me = lax.axis_index("dp")
    blocks = live.shape[1]
    row = lax.broadcasted_iota(i32, shape, axis)
    group = jnp.zeros(shape, i32)
    start = 0
    owners = []
    for b in range(blocks):
        owner = lax.div(slots[variants[me, b]], pool)
        nth = sum([(o == owner).astype(i32) for o in owners], jnp.int32(0))
        owners.append(owner)
        mine = lax.rem(me - owner + replicas, replicas) * capacity + nth
        group = jnp.where(row >= start, mine, group)
        start = start + live[0, b]
    return group


def shrink_kernel(variants, slots, live, *rest, replicas, capacity, pool, chunks):
    xs, downs, out = rest[:chunks], rest[chunks : chunks + replicas], rest[-1]
    depth = downs[0].shape[1]
    rank = out.shape[0]
    shape = (depth, live_total)
    group = row_groups(variants, slots, live, shape, 1, replicas, capacity, pool)
    nth = lax.broadcasted_iota(i32, shape, 0) // rank
    total = jnp.zeros(shape, f32)
    for o in range(replicas):
        part = jnp.zeros(shape, f32)
        start = 0
        for x in xs:
            stop = start + x.shape[1]
            part = part + lax.dot_general(
                downs[o][0, :, start:stop],
                x[...],
                (((1,), (1,)), ((), ())),
                preferred_element_type=f32,
            )
            start = stop
        total = total + jnp.where(group == o * capacity + nth, part, 0.0)
    result = total[:rank]
    for m in range(1, capacity):
        result = result + total[m * rank : (m + 1) * rank]
    out[...] = result


def shrink(variants, slots, live, xs, factors, capacity, pool):
    replicas = len(factors)
    depth, width = factors[0].shape[1:]
    rank = depth // capacity
    whole = pl.BlockSpec(memory_space=pltpu.VMEM)
    down = pl.BlockSpec((1, depth, width), lambda i: (0, 0, 0))
    return pl.pallas_call(
        functools.partial(
            shrink_kernel, replicas=replicas, capacity=capacity, pool=pool, chunks=len(xs)
        ),
        grid=(1,),
        in_specs=[smem] * 3
        + [pl.BlockSpec(x.shape, lambda i: (0, 0)) for x in xs]
        + [down] * replicas,
        out_specs=pl.BlockSpec((rank, live_total), lambda i: (0, 0)),
        out_shape=jax.ShapeDtypeStruct((rank, live_total), f32),
        compiler_params=params(),
        cost_estimate=cost(),
        name="shrink",
    )(variants, slots, live, *xs, *factors)


def project_kernel(*refs, groups, certain, has_total, delta, last, replicas, capacity, pool):
    refs = list(refs)
    meta, variants, slots, live = refs[:4]
    refs = refs[4:]
    total = refs.pop(0) if has_total else None
    xs = [[refs.pop(0) for _ in range(g)] for g in groups]
    ws = [refs.pop(0) for _ in groups]
    low = refs.pop(0) if delta else None
    ups = [refs.pop(0) for _ in range(replicas)] if delta else None
    out = refs.pop(0)
    spread = refs.pop(0) if delta else None
    held, hot = (refs.pop(0), refs.pop(0)) if last else (out, None)

    if delta or last:

        @pl.when(pl.program_id(0) == 0)
        def _():
            if last:
                hot[...] = one_hot(live, out.shape[0], 0)
            if delta:
                depth = ups[0].shape[1]
                shape = (live_total, depth)
                group = row_groups(variants, slots, live, shape, 0, replicas, capacity, pool)
                nth = lax.broadcasted_iota(i32, shape, 1) // (depth // capacity)
                wide = jnp.concatenate([low[...]] * capacity, axis=1) * adapter_scale
                for o in range(replicas):
                    mine = jnp.where(group == o * capacity + nth, wide, 0.0)
                    spread[:, o * depth : (o + 1) * depth] = mine.astype(bf16)

    def product(s):
        x = xs[s][0][...]
        for other in xs[s][1:]:
            x = x + other[...]
        return jnp.dot(x, ws[s][...], preferred_element_type=f32)

    sure = [s for s in range(len(groups)) if s in certain]
    value = total[...] if has_total else None
    for s in sure:
        value = product(s) if value is None else value + product(s)
    if delta:
        depth = ups[0].shape[1]
        for o in range(replicas):
            value = value + jnp.dot(
                spread[:, o * depth : (o + 1) * depth], ups[o][0], preferred_element_type=f32
            )
    if len(sure) == len(groups) and last:
        result = value.astype(bf16)
    else:
        held[...] = value
        for s in range(len(groups)):
            if s not in sure:

                @pl.when(meta[2 * s + 1] > 0)
                def _(s=s):
                    held[...] += product(s)

        result = held[...].astype(bf16) if last else None
    if last:
        out[...] = jnp.dot(hot[...], result, preferred_element_type=f32).astype(bf16)


def project(meta, ints, total, xs, weight, sizes, certain, low=None, factors=None, rows=None):
    replicas, capacity, pool = sizes
    columns = weight.shape[1]
    tile = min(column_tile, columns)
    in_specs = [smem] * 3
    args = list(ints)
    if total is not None:
        in_specs.append(pl.BlockSpec((live_total, tile), lambda i, m: (0, i)))
        args.append(total)
    for group in xs:
        for x in group:
            in_specs.append(pl.BlockSpec(x.shape, lambda i, m: (0, 0)))
            args.append(x)
    for s, group in enumerate(xs):
        k = group[0].shape[1]
        in_specs.append(pl.BlockSpec((k, tile), lambda i, m, s=s: (m[2 * s], i)))
        args.append(weight)
    scratch = []
    if low is not None:
        in_specs.append(pl.BlockSpec(low.shape, lambda i, m: (0, 0)))
        args.append(low)
        depth = factors[0].shape[1]
        for u in factors:
            in_specs.append(pl.BlockSpec((1, depth, tile), lambda i, m: (1, 0, i)))
            args.append(u)
        scratch.append(pltpu.VMEM((live_total, replicas * depth), bf16))
    if rows is None:
        out = jax.ShapeDtypeStruct((live_total, columns), f32)
        out_spec = pl.BlockSpec((live_total, tile), lambda i, m: (0, i))
    else:
        out = jax.ShapeDtypeStruct((rows, columns), bf16)
        out_spec = pl.BlockSpec((rows, tile), lambda i, m: (0, i))
        scratch += [pltpu.VMEM((live_total, tile), f32), pltpu.VMEM((rows, live_total), bf16)]
    return pl.pallas_call(
        functools.partial(
            project_kernel,
            groups=tuple(len(g) for g in xs),
            certain=certain,
            has_total=total is not None,
            delta=low is not None,
            last=rows is not None,
            replicas=replicas,
            capacity=capacity,
            pool=pool,
        ),
        grid_spec=pltpu.PrefetchScalarGridSpec(
            num_scalar_prefetch=1,
            grid=(columns // tile,),
            in_specs=in_specs,
            out_specs=out_spec,
            scratch_shapes=scratch,
        ),
        out_shape=out,
        compiler_params=params(),
        cost_estimate=cost(1 if low is None else 40_000_000_000),
        name="project",
    )(meta, *args)


def shards(
    hidden,
    query_weight,
    adapter_down,
    adapter_up,
    block_variant_index,
    variant_pool_slot,
    block_live_count,
):
    replicas = lax.axis_size("dp")
    tensor = lax.axis_size("tensor")
    place = lax.axis_index("tensor")
    pool = adapter_down.shape[0]
    blocks = block_variant_index.shape[1]
    rows, width = hidden.shape
    capacity = (blocks + replicas - 1) // replicas
    piece = min(chunk_width, width)
    chunks = width // piece
    ints = (block_variant_index, variant_pool_slot, block_live_count)
    sizes = (replicas, capacity, pool)

    def after(values, *events):
        return lax.optimization_barrier((values, events))[0]

    def source(step):
        return jnp.where(place >= step, place - step, jnp.minimum(place + step, tensor - 1))

    def meta(items):
        pairs = []
        for device, j, there in items:
            pairs += [device * chunks + j, there]
        return jnp.stack([jnp.asarray(p, i32) for p in pairs])

    def move(x, way, step):
        if way > 0:
            pairs = [(i, i + 1) for i in range(step - 1, tensor - 1)]
        else:
            pairs = [(i, i - 1) for i in range(1, tensor - step + 1)]
        return lax.ppermute(x, "tensor", pairs)

    def send(x, step):
        pairs = [(i, (i + step) % replicas) for i in range(replicas)]
        return lax.ppermute(x, "dp", pairs)

    one = jnp.int32(1)

    def arrivals(step, js):
        items, xs = [], []
        for j in js:
            if 2 * step >= tensor:
                items.append((source(step), j, one))
                xs.append((right[step][j], left[step][j]))
            else:
                items.append((jnp.maximum(place - step, 0), j, (place >= step).astype(i32)))
                xs.append((right[step][j],))
                behind = place + step
                items.append((jnp.minimum(behind, tensor - 1), j, (behind < tensor).astype(i32)))
                xs.append((left[step][j],))
        return items, xs

    def add(total, items, xs, **more):
        certain = tuple(s for s, item in enumerate(items) if item[2] is one)
        return project(meta(items), ints, total, xs, query_weight, sizes, certain, **more)

    own, factors = prepare(
        ints, hidden, adapter_down, adapter_up, (piece,) * chunks, replicas, capacity
    )
    right, left = [own], [own]

    def pass_on(first=(), final=()):
        step = len(right)
        for w, moved in ((1, right), (-1, left)):
            xs = list(moved[-1])
            xs[0] = after(xs[0], *first)
            xs[-1] = after(xs[-1], *final)
            moved.append([move(x, w, step) for x in xs])

    pass_on()
    items = [(place, j, one) for j in range(chunks)]
    own_total = add(None, items, [(x,) for x in own])

    got = [factors[0], send(factors[1], 1)]
    for step in range(2, replicas):
        got.append(send(after(factors[step], got[-1]), step))

    total = own_total
    firsts = []
    for j in range(chunks):
        total = add(total, *arrivals(1, [j]))
        firsts.append(total)
    partial = shrink(*ints[:2], after(ints[2], total), own, got, capacity, pool)

    late = ([], [])
    for step in range(2, tensor - 1):
        pass_on(*([[own_total], firsts[:1]] if step == 2 else []))
        total = add(total, *arrivals(step, range(max(chunks - 1, 1))))
        if chunks > 1:
            items, xs = arrivals(step, [chunks - 1])
            late = (late[0] + items, late[1] + xs)

    def pick(j, *events):
        return jnp.where(place == 1, after(left[-1][j], *events), after(right[-1][j], *events))

    ends = [(tensor - 2, tensor - 1), (1, 0)]
    source_end = jnp.where(place > 0, 0, tensor - 1)
    first_pick = pick(0, partial)

    low = hopped = partial
    for step in range(1, tensor):
        pairs = [(step - 1, step), (tensor - step, tensor - step - 1)]
        came = lax.ppermute(hopped, "tensor", pairs)
        if step == tensor - 2:
            came = after(came, first_pick)
        low = low + came
        if step < tensor - 1:
            hopped = partial + came
    low = low.astype(bf16).astype(f32).T

    final = []
    for j in range(chunks):
        x = first_pick if j == 0 else pick(j, hopped, total)
        final.append(lax.ppermute(x, "tensor", ends))
    for j in range(chunks):
        more = {"rows": rows} if j == chunks - 1 else {}
        items, xs = [(source_end, j, one)], [(final[j],)]
        if j == max(chunks - 2, 0):
            more.update(low=low, factors=got)
            items, xs = late[0] + items, late[1] + xs
        total = add(total, items, xs, **more)
    return total


def solution(mesh):
    return jax.shard_map(
        shards,
        mesh=mesh,
        in_specs=(
            P(("groups", "dp"), "tensor"),
            P(None, "tensor"),
            P("dp", None, "tensor"),
            P("dp", None, "tensor"),
            P("groups", None),
            P("groups"),
            P(("groups", "dp"), None),
        ),
        out_specs=P(("groups", "dp"), "tensor"),
        check_vma=False,
    )
```

```python
import functools

import jax
import jax.numpy as jnp
from jax import lax
from jax.experimental import pallas as pl
from jax.experimental.pallas import tpu as pltpu
from jax.sharding import PartitionSpec as P

adapter_scale = 2.0
live_total = 576
column_tile = 512
vmem_bytes = 62 * 1024 * 1024
bf16, f32, i32 = jnp.bfloat16, jnp.float32, jnp.int32

smem = pl.BlockSpec(memory_space=pltpu.SMEM)
hbm = pl.BlockSpec(memory_space=pl.ANY)


def params():
    return pltpu.CompilerParams(vmem_limit_bytes=vmem_bytes)


def cost(flops=1):
    return pl.CostEstimate(flops=flops, bytes_accessed=1, transcendentals=0)


def one_hot(live, rows, axis):
    blocks = live.shape[1]
    block = rows // blocks
    flat = (1, rows) if axis else (rows, 1)
    row = lax.broadcasted_iota(i32, flat, axis)
    place = jnp.full(flat, -1, i32)
    start = 0
    for b in range(blocks):
        inside = row - b * block
        here = (inside >= 0) & (inside < live[0, b])
        place = jnp.where(here, inside + start, place)
        start = start + live[0, b]
    shape = (live_total, rows) if axis else (rows, live_total)
    return (lax.broadcasted_iota(i32, shape, 1 - axis) == place).astype(f32).astype(bf16)


def prepare_kernel(
    variants, slots, live, x, down, up, packed, *rest, steps, replicas, capacity, blocks
):
    picked, sems = rest[:-1], rest[-1]
    pool, rank = down.shape[0], down.shape[1]
    me = lax.axis_index("dp")
    copies = []
    for step, place in zip(steps, picked):
        target = lax.rem(me + step, replicas)
        seen = jnp.int32(0)
        index = [jnp.int32(0)] * capacity
        for b in range(blocks):
            slot = slots[variants[target, b]]
            owner = lax.div(slot, pool)
            mine = owner == me
            for m in range(capacity):
                index[m] = jnp.where(mine & (seen == m), slot - owner * pool, index[m])
            seen = seen + mine.astype(i32)
        for m in range(capacity):
            for kind, pooled in enumerate((down, up)):
                copies.append(
                    pltpu.make_async_copy(
                        pooled.at[index[m]],
                        place.at[kind, m * rank : (m + 1) * rank],
                        sems.at[len(copies)],
                    )
                )
                copies[-1].start()
    hot = one_hot(live, x.shape[0], 1)
    packed[...] = jnp.dot(hot, x[...], preferred_element_type=f32).astype(bf16)
    for copy in copies:
        copy.wait()


def prepare(ints, hidden, down, up, part, parts, steps, replicas, capacity):
    rows, features = hidden.shape
    width = features // parts
    depth = capacity * down.shape[1]
    outs = [jax.ShapeDtypeStruct((live_total, width), bf16)]
    outs += [jax.ShapeDtypeStruct((2, depth, features), bf16)] * len(steps)
    results = pl.pallas_call(
        functools.partial(
            prepare_kernel,
            steps=steps,
            replicas=replicas,
            capacity=capacity,
            blocks=ints[0].shape[1],
        ),
        grid=(1,),
        in_specs=[smem] * 3 + [pl.BlockSpec((rows, width), lambda i: (0, part)), hbm, hbm],
        out_specs=[pl.BlockSpec(o.shape, lambda i, r=len(o.shape): (0,) * r) for o in outs],
        out_shape=outs,
        scratch_shapes=[pltpu.SemaphoreType.DMA((len(steps) * capacity * 2,))],
        compiler_params=params(),
        cost_estimate=cost(),
        name="prepare",
    )(*ints, hidden, down, up)
    return results[0], results[1:]


def row_groups(variants, slots, live, shape, axis, replicas, capacity, pool):
    me = lax.axis_index("dp")
    blocks = live.shape[1]
    row = lax.broadcasted_iota(i32, shape, axis)
    group = jnp.zeros(shape, i32)
    start = 0
    owners = []
    for b in range(blocks):
        owner = lax.div(slots[variants[me, b]], pool)
        nth = sum([(o == owner).astype(i32) for o in owners], jnp.int32(0))
        owners.append(owner)
        mine = lax.rem(me - owner + replicas, replicas) * capacity + nth
        group = jnp.where(row >= start, mine, group)
        start = start + live[0, b]
    return group


def shrink_kernel(variants, slots, live, *rest, replicas, capacity, pool, chunks):
    xs, downs, out = rest[:chunks], rest[chunks : chunks + replicas], rest[-1]
    depth = downs[0].shape[1]
    rank = out.shape[0]
    shape = (depth, live_total)
    group = row_groups(variants, slots, live, shape, 1, replicas, capacity, pool)
    nth = lax.broadcasted_iota(i32, shape, 0) // rank
    total = jnp.zeros(shape, f32)
    for o in range(replicas):
        part = jnp.zeros(shape, f32)
        start = 0
        for x in xs:
            stop = start + x.shape[1]
            part = part + lax.dot_general(
                downs[o][0, :, start:stop],
                x[...],
                (((1,), (1,)), ((), ())),
                preferred_element_type=f32,
            )
            start = stop
        total = total + jnp.where(group == o * capacity + nth, part, 0.0)
    result = total[:rank]
    for m in range(1, capacity):
        result = result + total[m * rank : (m + 1) * rank]
    out[...] = result


def shrink(variants, slots, live, xs, factors, capacity, pool):
    replicas = len(factors)
    depth, width = factors[0].shape[1:]
    rank = depth // capacity
    whole = pl.BlockSpec(memory_space=pltpu.VMEM)
    down = pl.BlockSpec((1, depth, width), lambda i: (0, 0, 0))
    return pl.pallas_call(
        functools.partial(
            shrink_kernel, replicas=replicas, capacity=capacity, pool=pool, chunks=len(xs)
        ),
        grid=(1,),
        in_specs=[smem] * 3
        + [pl.BlockSpec(x.shape, lambda i: (0, 0)) for x in xs]
        + [down] * replicas,
        out_specs=pl.BlockSpec((rank, live_total), lambda i: (0, 0)),
        out_shape=jax.ShapeDtypeStruct((rank, live_total), f32),
        compiler_params=params(),
        cost_estimate=cost(),
        name="shrink",
    )(variants, slots, live, *xs, *factors)


def project_kernel(*refs, groups, has_total, delta, last, replicas, capacity, pool):
    refs = list(refs)
    meta, variants, slots, live = refs[:4]
    refs = refs[4:]
    total = refs.pop(0) if has_total else None
    xs = [[refs.pop(0) for _ in range(g)] for g in groups]
    ws = [refs.pop(0) for _ in groups]
    low = refs.pop(0) if delta else None
    ups = [refs.pop(0) for _ in range(replicas)] if delta else None
    out = refs.pop(0)
    spread = refs.pop(0) if delta else None
    hot = refs.pop(0) if last else None

    if delta or last:

        @pl.when(pl.program_id(0) == 0)
        def _():
            if last:
                hot[...] = one_hot(live, out.shape[0], 0)
            if delta:
                depth = ups[0].shape[1]
                shape = (live_total, depth)
                group = row_groups(variants, slots, live, shape, 0, replicas, capacity, pool)
                nth = lax.broadcasted_iota(i32, shape, 1) // (depth // capacity)
                wide = jnp.concatenate([low[...]] * capacity, axis=1) * adapter_scale
                for o in range(replicas):
                    mine = jnp.where(group == o * capacity + nth, wide, 0.0)
                    spread[:, o * depth : (o + 1) * depth] = mine.astype(bf16)

    def product(s):
        x = xs[s][0][...]
        for other in xs[s][1:]:
            x = x + other[...]
        return jnp.dot(x, ws[s][...], preferred_element_type=f32)

    value = total[...] if has_total else None
    for s in range(len(groups)):
        value = product(s) if value is None else value + product(s)
    if delta:
        depth = ups[0].shape[1]
        for o in range(replicas):
            value = value + jnp.dot(
                spread[:, o * depth : (o + 1) * depth], ups[o][0], preferred_element_type=f32
            )
    if last:
        value = jnp.dot(hot[...], value.astype(bf16), preferred_element_type=f32)
    out[...] = value.astype(out.dtype)


def project(meta, ints, total, xs, weight, sizes, low=None, factors=None, rows=None, flops=1):
    replicas, capacity, pool = sizes
    columns = weight.shape[1]
    tile = min(column_tile, columns)
    in_specs = [smem] * 3
    args = list(ints)
    if total is not None:
        in_specs.append(pl.BlockSpec((live_total, tile), lambda i, m: (0, i)))
        args.append(total)
    for group in xs:
        for x in group:
            in_specs.append(pl.BlockSpec(x.shape, lambda i, m: (0, 0)))
            args.append(x)
    for s, group in enumerate(xs):
        k = group[0].shape[1]
        in_specs.append(pl.BlockSpec((k, tile), lambda i, m, s=s: (m[s], i)))
        args.append(weight)
    scratch = []
    if low is not None:
        in_specs.append(pl.BlockSpec(low.shape, lambda i, m: (0, 0)))
        args.append(low)
        depth = factors[0].shape[1]
        for u in factors:
            in_specs.append(pl.BlockSpec((1, depth, tile), lambda i, m: (1, 0, i)))
            args.append(u)
        scratch.append(pltpu.VMEM((live_total, replicas * depth), bf16))
    if rows is None:
        out = jax.ShapeDtypeStruct((live_total, columns), f32)
        out_spec = pl.BlockSpec((live_total, tile), lambda i, m: (0, i))
    else:
        out = jax.ShapeDtypeStruct((rows, columns), bf16)
        out_spec = pl.BlockSpec((rows, tile), lambda i, m: (0, i))
        scratch.append(pltpu.VMEM((rows, live_total), bf16))
    return pl.pallas_call(
        functools.partial(
            project_kernel,
            groups=tuple(len(g) for g in xs),
            has_total=total is not None,
            delta=low is not None,
            last=rows is not None,
            replicas=replicas,
            capacity=capacity,
            pool=pool,
        ),
        grid_spec=pltpu.PrefetchScalarGridSpec(
            num_scalar_prefetch=1,
            grid=(columns // tile,),
            in_specs=in_specs,
            out_specs=out_spec,
            scratch_shapes=scratch,
        ),
        out_shape=out,
        compiler_params=params(),
        cost_estimate=cost(flops),
        name="project",
    )(meta, *args)


def shards(
    hidden,
    query_weight,
    adapter_down,
    adapter_up,
    block_variant_index,
    variant_pool_slot,
    block_live_count,
):
    replicas = lax.axis_size("dp")
    tensor = lax.axis_size("tensor")
    place = lax.axis_index("tensor")
    pool = adapter_down.shape[0]
    blocks = block_variant_index.shape[1]
    rows, width = hidden.shape
    capacity = (blocks + replicas - 1) // replicas
    piece = width // 2
    ints = (block_variant_index, variant_pool_slot, block_live_count)
    sizes = (replicas, capacity, pool)

    def after(values, *events):
        return lax.optimization_barrier((values, events))[0]

    def add(total, items, **more):
        xs = [item[2] for item in items]
        meta = [item[0] * (width // item[2][0].shape[1]) + item[1] for item in items]
        meta = jnp.stack([jnp.asarray(m, i32) for m in meta])
        return project(meta, ints, total, xs, query_weight, sizes, **more)

    pools = (hidden, adapter_down, adapter_up)
    own0, (next_factors,) = prepare(ints, *pools, 0, 2, (1,), replicas, capacity)
    steps = (0,) + tuple(range(2, replicas))
    own1, factors = prepare(ints, *pools, 1, 2, steps, replicas, capacity)
    factors = [factors[0], next_factors, *factors[1:]]
    own = (own0, own1)

    def send(x, step):
        pairs = [(i, (i + step) % replicas) for i in range(replicas)]
        return lax.ppermute(x, "dp", pairs)

    own_total = add(None, [(place, j, (own[j],)) for j in range(2)])
    got = [factors[0], send(factors[1], 1)]
    for step in range(2, replicas):
        events = got[-1:] if step < replicas - 1 else [got[-1], own_total]
        got.append(send(after(factors[step], *events), step))

    if tensor != 4:
        gathered = [lax.all_gather(x, "tensor", axis=0) for x in own]
        low = lax.psum(shrink(*ints, own, got, capacity, pool), "tensor")
        low = low.astype(bf16).astype(f32).T
        total = own_total
        for step in range(1, tensor):
            device = (place + step) % tensor
            xs = [lax.dynamic_index_in_dim(x, device, 0, keepdims=False) for x in gathered]
            items = [(device, j, (xs[j],)) for j in range(2)]
            more = {"rows": rows, "low": low, "factors": got} if step == tensor - 1 else {}
            total = add(total, items, **more)
        return total

    def pairs(x):
        return lax.ppermute(x, "tensor", [(0, 1), (1, 0), (2, 3), (3, 2)])

    def middle(x):
        return lax.ppermute(x, "tensor", [(1, 2), (2, 1)])

    def outward(x):
        return lax.ppermute(x, "tensor", [(1, 0), (2, 3)])

    near = place ^ 1
    far = jnp.where(place < 2, 2, 1)
    farthest = jnp.where(place < 2, 3, 0)

    x1 = [pairs(x) for x in own]
    y1 = [middle(x) for x in own]
    near_total = add(own_total, [(near, 0, (x1[0],))])
    total = add(near_total, [(near, 1, (x1[1],))])
    partial = shrink(*ints[:2], after(ints[2], total), own, got, capacity, pool)

    x2_0, y2_0 = outward(y1[0]), middle(x1[0])
    x2_1, y2_1 = outward(after(y1[1], near_total)), middle(after(x1[1], near_total))
    total = add(total, [(far, 0, (y1[0], x2_0))], flops=20_000_000_000)

    inward = lax.ppermute(partial, "tensor", [(0, 1), (3, 2)])
    across = middle(partial + inward)
    across = after(across, y2_0)
    hopped = partial + across
    outer = outward(hopped)
    low = (partial + inward + across + outer).astype(bf16).astype(f32).T

    x3_0 = outward(after(y2_0, partial))
    y2_1 = after(y2_1, hopped, total)
    half = piece // 2
    halves = [y2_1[:, :half], y2_1[:, half:]]
    x3_1 = [outward(h) for h in halves]

    items = [(far, 1, (y1[1], x2_1)), (farthest, 0, (y2_0, x3_0))]
    total = add(total, items, low=low, factors=got, flops=40_000_000_000)
    total = add(total, [(farthest, 2, (halves[0], x3_1[0]))])
    return add(total, [(farthest, 3, (halves[1], x3_1[1]))], rows=rows)


def solution(mesh):
    return jax.shard_map(
        shards,
        mesh=mesh,
        in_specs=(
            P(("groups", "dp"), "tensor"),
            P(None, "tensor"),
            P("dp", None, "tensor"),
            P("dp", None, "tensor"),
            P("groups", None),
            P("groups"),
            P(("groups", "dp"), None),
        ),
        out_specs=P(("groups", "dp"), "tensor"),
        check_vma=False,
    )
```

```python
import functools

import jax
import jax.numpy as jnp
from jax import lax
from jax.experimental import pallas as pl
from jax.experimental.pallas import tpu as pltpu
from jax.sharding import PartitionSpec as P

adapter_scale = 2.0
live_total = 576
column_tile = 512
vmem_bytes = 62 * 1024 * 1024
bf16, f32, i32 = jnp.bfloat16, jnp.float32, jnp.int32

smem = pl.BlockSpec(memory_space=pltpu.SMEM)
hbm = pl.BlockSpec(memory_space=pl.ANY)


def params():
    return pltpu.CompilerParams(vmem_limit_bytes=vmem_bytes)


def cost(flops=1):
    return pl.CostEstimate(flops=flops, bytes_accessed=1, transcendentals=0)


def one_hot(live, rows, axis):
    blocks = live.shape[1]
    block = rows // blocks
    flat = (1, rows) if axis else (rows, 1)
    row = lax.broadcasted_iota(i32, flat, axis)
    place = jnp.full(flat, -1, i32)
    start = 0
    for b in range(blocks):
        inside = row - b * block
        here = (inside >= 0) & (inside < live[0, b])
        place = jnp.where(here, inside + start, place)
        start = start + live[0, b]
    shape = (live_total, rows) if axis else (rows, live_total)
    return (lax.broadcasted_iota(i32, shape, 1 - axis) == place).astype(f32).astype(bf16)


def prepare_kernel(
    variants, slots, live, x, down, up, packed, *rest, steps, replicas, capacity, blocks
):
    picked, sems = rest[:-1], rest[-1]
    pool, rank = down.shape[0], down.shape[1]
    me = lax.axis_index("dp")
    copies = []
    for step, place in zip(steps, picked):
        target = lax.rem(me + step, replicas)
        seen = jnp.int32(0)
        index = [jnp.int32(0)] * capacity
        for b in range(blocks):
            slot = slots[variants[target, b]]
            owner = lax.div(slot, pool)
            mine = owner == me
            for m in range(capacity):
                index[m] = jnp.where(mine & (seen == m), slot - owner * pool, index[m])
            seen = seen + mine.astype(i32)
        for m in range(capacity):
            for kind, pooled in enumerate((down, up)):
                copies.append(
                    pltpu.make_async_copy(
                        pooled.at[index[m]],
                        place.at[kind, m * rank : (m + 1) * rank],
                        sems.at[len(copies)],
                    )
                )
                copies[-1].start()
    hot = one_hot(live, x.shape[0], 1)
    packed[...] = jnp.dot(hot, x[...], preferred_element_type=f32).astype(bf16)
    for copy in copies:
        copy.wait()


def prepare(ints, hidden, down, up, part, parts, steps, replicas, capacity):
    rows, features = hidden.shape
    width = features // parts
    depth = capacity * down.shape[1]
    outs = [jax.ShapeDtypeStruct((live_total, width), bf16)]
    outs += [jax.ShapeDtypeStruct((2, depth, features), bf16)] * len(steps)
    results = pl.pallas_call(
        functools.partial(
            prepare_kernel,
            steps=steps,
            replicas=replicas,
            capacity=capacity,
            blocks=ints[0].shape[1],
        ),
        grid=(1,),
        in_specs=[smem] * 3 + [pl.BlockSpec((rows, width), lambda i: (0, part)), hbm, hbm],
        out_specs=[pl.BlockSpec(o.shape, lambda i, r=len(o.shape): (0,) * r) for o in outs],
        out_shape=outs,
        scratch_shapes=[pltpu.SemaphoreType.DMA((len(steps) * capacity * 2,))],
        compiler_params=params(),
        cost_estimate=cost(),
        name="prepare",
    )(*ints, hidden, down, up)
    return results[0], results[1:]


def row_groups(variants, slots, live, shape, axis, replicas, capacity, pool):
    me = lax.axis_index("dp")
    blocks = live.shape[1]
    row = lax.broadcasted_iota(i32, shape, axis)
    group = jnp.zeros(shape, i32)
    start = 0
    owners = []
    for b in range(blocks):
        owner = lax.div(slots[variants[me, b]], pool)
        nth = sum([(o == owner).astype(i32) for o in owners], jnp.int32(0))
        owners.append(owner)
        mine = lax.rem(me - owner + replicas, replicas) * capacity + nth
        group = jnp.where(row >= start, mine, group)
        start = start + live[0, b]
    return group


def shrink_kernel(variants, slots, live, *rest, replicas, capacity, pool, chunks):
    xs, downs, out = rest[:chunks], rest[chunks : chunks + replicas], rest[-1]
    depth = downs[0].shape[1]
    rank = out.shape[0]
    shape = (depth, live_total)
    group = row_groups(variants, slots, live, shape, 1, replicas, capacity, pool)
    nth = lax.broadcasted_iota(i32, shape, 0) // rank
    total = jnp.zeros(shape, f32)
    for o in range(replicas):
        part = jnp.zeros(shape, f32)
        start = 0
        for x in xs:
            stop = start + x.shape[1]
            part = part + lax.dot_general(
                downs[o][0, :, start:stop],
                x[...],
                (((1,), (1,)), ((), ())),
                preferred_element_type=f32,
            )
            start = stop
        total = total + jnp.where(group == o * capacity + nth, part, 0.0)
    result = total[:rank]
    for m in range(1, capacity):
        result = result + total[m * rank : (m + 1) * rank]
    out[...] = result


def shrink(variants, slots, live, xs, factors, capacity, pool):
    replicas = len(factors)
    depth, width = factors[0].shape[1:]
    rank = depth // capacity
    whole = pl.BlockSpec(memory_space=pltpu.VMEM)
    down = pl.BlockSpec((1, depth, width), lambda i: (0, 0, 0))
    return pl.pallas_call(
        functools.partial(
            shrink_kernel, replicas=replicas, capacity=capacity, pool=pool, chunks=len(xs)
        ),
        grid=(1,),
        in_specs=[smem] * 3
        + [pl.BlockSpec(x.shape, lambda i: (0, 0)) for x in xs]
        + [down] * replicas,
        out_specs=pl.BlockSpec((rank, live_total), lambda i: (0, 0)),
        out_shape=jax.ShapeDtypeStruct((rank, live_total), f32),
        compiler_params=params(),
        cost_estimate=cost(),
        name="shrink",
    )(variants, slots, live, *xs, *factors)


def project_kernel(*refs, groups, has_total, delta, last, replicas, capacity, pool):
    refs = list(refs)
    meta, variants, slots, live = refs[:4]
    refs = refs[4:]
    total = refs.pop(0) if has_total else None
    xs = [[refs.pop(0) for _ in range(g)] for g in groups]
    ws = [refs.pop(0) for _ in groups]
    low = refs.pop(0) if delta else None
    ups = [refs.pop(0) for _ in range(replicas)] if delta else None
    out = refs.pop(0)
    spread = refs.pop(0) if delta else None
    hot = refs.pop(0) if last else None

    if delta or last:

        @pl.when(pl.program_id(0) == 0)
        def _():
            if last:
                hot[...] = one_hot(live, out.shape[0], 0)
            if delta:
                depth = ups[0].shape[1]
                shape = (live_total, depth)
                group = row_groups(variants, slots, live, shape, 0, replicas, capacity, pool)
                nth = lax.broadcasted_iota(i32, shape, 1) // (depth // capacity)
                wide = jnp.concatenate([low[...]] * capacity, axis=1) * adapter_scale
                for o in range(replicas):
                    mine = jnp.where(group == o * capacity + nth, wide, 0.0)
                    spread[:, o * depth : (o + 1) * depth] = mine.astype(bf16)

    def product(s):
        x = xs[s][0][...]
        for other in xs[s][1:]:
            x = x + other[...]
        return jnp.dot(x, ws[s][...], preferred_element_type=f32)

    value = total[...] if has_total else None
    for s in range(len(groups)):
        value = product(s) if value is None else value + product(s)
    if delta:
        depth = ups[0].shape[1]
        for o in range(replicas):
            value = value + jnp.dot(
                spread[:, o * depth : (o + 1) * depth], ups[o][0], preferred_element_type=f32
            )
    if last:
        value = jnp.dot(hot[...], value.astype(bf16), preferred_element_type=f32)
    out[...] = value.astype(out.dtype)


def project(meta, ints, total, xs, weight, sizes, low=None, factors=None, rows=None, flops=1):
    replicas, capacity, pool = sizes
    columns = weight.shape[1]
    tile = min(column_tile, columns)
    in_specs = [smem] * 3
    args = list(ints)
    if total is not None:
        in_specs.append(pl.BlockSpec((live_total, tile), lambda i, m: (0, i)))
        args.append(total)
    for group in xs:
        for x in group:
            in_specs.append(pl.BlockSpec(x.shape, lambda i, m: (0, 0)))
            args.append(x)
    for s, group in enumerate(xs):
        k = group[0].shape[1]
        in_specs.append(pl.BlockSpec((k, tile), lambda i, m, s=s: (m[s], i)))
        args.append(weight)
    scratch = []
    if low is not None:
        in_specs.append(pl.BlockSpec(low.shape, lambda i, m: (0, 0)))
        args.append(low)
        depth = factors[0].shape[1]
        for u in factors:
            in_specs.append(pl.BlockSpec((1, depth, tile), lambda i, m: (1, 0, i)))
            args.append(u)
        scratch.append(pltpu.VMEM((live_total, replicas * depth), bf16))
    if rows is None:
        out = jax.ShapeDtypeStruct((live_total, columns), f32)
        out_spec = pl.BlockSpec((live_total, tile), lambda i, m: (0, i))
    else:
        out = jax.ShapeDtypeStruct((rows, columns), bf16)
        out_spec = pl.BlockSpec((rows, tile), lambda i, m: (0, i))
        scratch.append(pltpu.VMEM((rows, live_total), bf16))
    return pl.pallas_call(
        functools.partial(
            project_kernel,
            groups=tuple(len(g) for g in xs),
            has_total=total is not None,
            delta=low is not None,
            last=rows is not None,
            replicas=replicas,
            capacity=capacity,
            pool=pool,
        ),
        grid_spec=pltpu.PrefetchScalarGridSpec(
            num_scalar_prefetch=1,
            grid=(columns // tile,),
            in_specs=in_specs,
            out_specs=out_spec,
            scratch_shapes=scratch,
        ),
        out_shape=out,
        compiler_params=params(),
        cost_estimate=cost(flops),
        name="project",
    )(meta, *args)


def shards(
    hidden,
    query_weight,
    adapter_down,
    adapter_up,
    block_variant_index,
    variant_pool_slot,
    block_live_count,
):
    replicas = lax.axis_size("dp")
    tensor = lax.axis_size("tensor")
    place = lax.axis_index("tensor")
    pool = adapter_down.shape[0]
    blocks = block_variant_index.shape[1]
    rows, width = hidden.shape
    capacity = (blocks + replicas - 1) // replicas
    piece = width // 2
    ints = (block_variant_index, variant_pool_slot, block_live_count)
    sizes = (replicas, capacity, pool)

    def after(values, *events):
        return lax.optimization_barrier((values, events))[0]

    def add(total, items, **more):
        xs = [item[2] for item in items]
        meta = [item[0] * (width // item[2][0].shape[1]) + item[1] for item in items]
        meta = jnp.stack([jnp.asarray(m, i32) for m in meta])
        return project(meta, ints, total, xs, query_weight, sizes, **more)

    pools = (hidden, adapter_down, adapter_up)
    own0, (next_factors,) = prepare(ints, *pools, 0, 2, (1,), replicas, capacity)
    steps = (0,) + tuple(range(2, replicas))
    own1, factors = prepare(ints, *pools, 1, 2, steps, replicas, capacity)
    factors = [factors[0], next_factors, *factors[1:]]
    own = (own0, own1)

    def send(x, step):
        pairs = [(i, (i + step) % replicas) for i in range(replicas)]
        return lax.ppermute(x, "dp", pairs)

    own_total = add(None, [(place, j, (own[j],)) for j in range(2)])
    got = [factors[0], send(factors[1], 1)]
    for step in range(2, replicas):
        events = got[-1:] if step < replicas - 1 else [got[-1], own_total]
        got.append(send(after(factors[step], *events), step))

    if tensor != 4:
        gathered = [lax.all_gather(x, "tensor", axis=0) for x in own]
        low = lax.psum(shrink(*ints, own, got, capacity, pool), "tensor")
        low = low.astype(bf16).astype(f32).T
        total = own_total
        for step in range(1, tensor):
            device = (place + step) % tensor
            xs = [lax.dynamic_index_in_dim(x, device, 0, keepdims=False) for x in gathered]
            items = [(device, j, (xs[j],)) for j in range(2)]
            more = {"rows": rows, "low": low, "factors": got} if step == tensor - 1 else {}
            total = add(total, items, **more)
        return total

    def pairs(x):
        return lax.ppermute(x, "tensor", [(0, 1), (1, 0), (2, 3), (3, 2)])

    def middle(x):
        return lax.ppermute(x, "tensor", [(1, 2), (2, 1)])

    def outward(x):
        return lax.ppermute(x, "tensor", [(1, 0), (2, 3)])

    near = place ^ 1
    far = jnp.where(place < 2, 2, 1)
    farthest = jnp.where(place < 2, 3, 0)

    x1 = [pairs(x) for x in own]
    y1 = [middle(x) for x in own]
    near_total = add(own_total, [(near, 0, (x1[0],))])
    total = add(near_total, [(near, 1, (x1[1],))])
    partial = shrink(*ints[:2], after(ints[2], total), own, got, capacity, pool)

    x2_0, y2_0 = outward(y1[0]), middle(x1[0])
    x2_1, y2_1 = outward(after(y1[1], near_total)), middle(after(x1[1], near_total))
    total = add(total, [(far, 0, (y1[0], x2_0))], flops=3_450_000_000)

    inward = lax.ppermute(partial, "tensor", [(0, 1), (3, 2)])
    across = middle(partial + inward)
    across = after(across, y2_0)
    hopped = partial + across
    outer = outward(hopped)
    low = (partial + inward + across + outer).astype(bf16).astype(f32).T

    x3_0 = outward(after(y2_0, partial))
    y2_1 = after(y2_1, hopped, total)
    half = piece // 2
    halves = [y2_1[:, :half], y2_1[:, half:]]
    x3_1 = [outward(h) for h in halves]

    items = [(far, 1, (y1[1], x2_1)), (farthest, 0, (y2_0, x3_0))]
    total = add(total, items, low=low, factors=got, flops=2_300_000_000)
    total = add(total, [(farthest, 2, (halves[0], x3_1[0]))], flops=1_150_000_000)
    return add(total, [(farthest, 3, (halves[1], x3_1[1]))], rows=rows)


def solution(mesh):
    return jax.shard_map(
        shards,
        mesh=mesh,
        in_specs=(
            P(("groups", "dp"), "tensor"),
            P(None, "tensor"),
            P("dp", None, "tensor"),
            P("dp", None, "tensor"),
            P("groups", None),
            P("groups"),
            P(("groups", "dp"), None),
        ),
        out_specs=P(("groups", "dp"), "tensor"),
        check_vma=False,
    )
```

```python
import functools

import jax
import jax.numpy as jnp
from jax import lax
from jax.experimental import pallas as pl
from jax.experimental.pallas import tpu as pltpu
from jax.sharding import PartitionSpec as P

adapter_scale = 2.0
live_total = 576
column_tile = 512
strip_width = 256
pack_strip = 512
vmem_bytes = 62 * 1024 * 1024
bf16, f32, i32 = jnp.bfloat16, jnp.float32, jnp.int32

smem = pl.BlockSpec(memory_space=pltpu.SMEM)
hbm = pl.BlockSpec(memory_space=pl.ANY)


def params():
    return pltpu.CompilerParams(vmem_limit_bytes=vmem_bytes)


def cost(flops=1):
    return pl.CostEstimate(flops=flops, bytes_accessed=1, transcendentals=0)


def one_hot(live, rows, axis):
    blocks = live.shape[1]
    block = rows // blocks
    flat = (1, rows) if axis else (rows, 1)
    row = lax.broadcasted_iota(i32, flat, axis)
    place = jnp.full(flat, -1, i32)
    start = 0
    for b in range(blocks):
        inside = row - b * block
        here = (inside >= 0) & (inside < live[0, b])
        place = jnp.where(here, inside + start, place)
        start = start + live[0, b]
    shape = (live_total, rows) if axis else (rows, live_total)
    return (lax.broadcasted_iota(i32, shape, 1 - axis) == place).astype(f32).astype(bf16)


def prepare_kernel(
    variants, slots, live, x, down, up, packed, *rest, steps, replicas, capacity, blocks
):
    picked, hot, sems = rest[:-2], rest[-2], rest[-1]
    pool, rank = down.shape[0], down.shape[1]

    def copies():
        me = lax.axis_index("dp")
        made = []
        for step, place in zip(steps, picked):
            target = lax.rem(me + step, replicas)
            seen = jnp.int32(0)
            index = [jnp.int32(0)] * capacity
            for b in range(blocks):
                slot = slots[variants[target, b]]
                owner = lax.div(slot, pool)
                mine = owner == me
                for m in range(capacity):
                    index[m] = jnp.where(mine & (seen == m), slot - owner * pool, index[m])
                seen = seen + mine.astype(i32)
            for m in range(capacity):
                for kind, pooled in enumerate((down, up)):
                    made.append(
                        pltpu.make_async_copy(
                            pooled.at[index[m]],
                            place.at[kind, m * rank : (m + 1) * rank],
                            sems.at[len(made)],
                        )
                    )
        return made

    @pl.when(pl.program_id(0) == 0)
    def _():
        for copy in copies():
            copy.start()
        hot[...] = one_hot(live, x.shape[0], 1)

    packed[...] = jnp.dot(hot[...], x[...], preferred_element_type=f32).astype(bf16)

    @pl.when(pl.program_id(0) == pl.num_programs(0) - 1)
    def _():
        for copy in copies():
            copy.wait()


def prepare(ints, hidden, down, up, part, parts, steps, replicas, capacity):
    rows, features = hidden.shape
    width = features // parts
    strip = min(pack_strip, width)
    strips = width // strip
    depth = capacity * down.shape[1]
    outs = [jax.ShapeDtypeStruct((live_total, width), bf16)]
    outs += [jax.ShapeDtypeStruct((2, depth, features), bf16)] * len(steps)
    results = pl.pallas_call(
        functools.partial(
            prepare_kernel,
            steps=steps,
            replicas=replicas,
            capacity=capacity,
            blocks=ints[0].shape[1],
        ),
        grid=(strips,),
        in_specs=[smem] * 3 + [pl.BlockSpec((rows, strip), lambda i: (0, part * strips + i)), hbm, hbm],
        out_specs=[pl.BlockSpec((live_total, strip), lambda i: (0, i))]
        + [pl.BlockSpec(o.shape, lambda i: (0, 0, 0)) for o in outs[1:]],
        out_shape=outs,
        scratch_shapes=[
            pltpu.VMEM((live_total, rows), bf16),
            pltpu.SemaphoreType.DMA((len(steps) * capacity * 2,)),
        ],
        compiler_params=params(),
        cost_estimate=cost(),
        name="prepare",
    )(*ints, hidden, down, up)
    return results[0], results[1:]


def row_groups(variants, slots, live, shape, axis, replicas, capacity, pool):
    me = lax.axis_index("dp")
    blocks = live.shape[1]
    row = lax.broadcasted_iota(i32, shape, axis)
    group = jnp.zeros(shape, i32)
    start = 0
    owners = []
    for b in range(blocks):
        owner = lax.div(slots[variants[me, b]], pool)
        nth = sum([(o == owner).astype(i32) for o in owners], jnp.int32(0))
        owners.append(owner)
        mine = lax.rem(me - owner + replicas, replicas) * capacity + nth
        group = jnp.where(row >= start, mine, group)
        start = start + live[0, b]
    return group


def shrink_kernel(variants, slots, live, *rest, replicas, capacity, pool, chunks):
    xs, downs, out = rest[:chunks], rest[chunks : chunks + replicas], rest[-1]
    depth = downs[0].shape[1]
    rank = out.shape[0]
    shape = (depth, live_total)
    group = row_groups(variants, slots, live, shape, 1, replicas, capacity, pool)
    nth = lax.broadcasted_iota(i32, shape, 0) // rank
    total = jnp.zeros(shape, f32)
    for o in range(replicas):
        part = jnp.zeros(shape, f32)
        start = 0
        for x in xs:
            stop = start + x.shape[1]
            part = part + lax.dot_general(
                downs[o][0, :, start:stop],
                x[...],
                (((1,), (1,)), ((), ())),
                preferred_element_type=f32,
            )
            start = stop
        total = total + jnp.where(group == o * capacity + nth, part, 0.0)
    result = total[:rank]
    for m in range(1, capacity):
        result = result + total[m * rank : (m + 1) * rank]
    out[...] = result


def shrink(variants, slots, live, xs, factors, capacity, pool):
    replicas = len(factors)
    depth, width = factors[0].shape[1:]
    rank = depth // capacity
    whole = pl.BlockSpec(memory_space=pltpu.VMEM)
    down = pl.BlockSpec((1, depth, width), lambda i: (0, 0, 0))
    return pl.pallas_call(
        functools.partial(
            shrink_kernel, replicas=replicas, capacity=capacity, pool=pool, chunks=len(xs)
        ),
        grid=(1,),
        in_specs=[smem] * 3
        + [pl.BlockSpec(x.shape, lambda i: (0, 0)) for x in xs]
        + [down] * replicas,
        out_specs=pl.BlockSpec((rank, live_total), lambda i: (0, 0)),
        out_shape=jax.ShapeDtypeStruct((rank, live_total), f32),
        compiler_params=params(),
        cost_estimate=cost(),
        name="shrink",
    )(variants, slots, live, *xs, *factors)


def project_kernel(*refs, groups, has_total, delta, last, replicas, capacity, pool):
    refs = list(refs)
    meta, variants, slots, live = refs[:4]
    refs = refs[4:]
    total = refs.pop(0) if has_total else None
    xs = [[refs.pop(0) for _ in range(g)] for g in groups]
    ws = [refs.pop(0) for _ in groups]
    low = refs.pop(0) if delta else None
    ups = [refs.pop(0) for _ in range(replicas)] if delta else None
    out = refs.pop(0)
    spread = refs.pop(0) if delta else None
    hot = refs.pop(0) if last else None

    if delta or last:

        @pl.when(pl.program_id(0) == 0)
        def _():
            if last:
                hot[...] = one_hot(live, out.shape[0], 0)
            if delta:
                depth = ups[0].shape[1]
                shape = (live_total, depth)
                group = row_groups(variants, slots, live, shape, 0, replicas, capacity, pool)
                nth = lax.broadcasted_iota(i32, shape, 1) // (depth // capacity)
                wide = jnp.concatenate([low[...]] * capacity, axis=1) * adapter_scale
                for o in range(replicas):
                    mine = jnp.where(group == o * capacity + nth, wide, 0.0)
                    spread[:, o * depth : (o + 1) * depth] = mine.astype(bf16)

    def product(s, columns):
        x = xs[s][0][...]
        for other in xs[s][1:]:
            x = x + other[...]
        return jnp.dot(x, ws[s][:, columns], preferred_element_type=f32)

    def work(columns):
        value = total[:, columns] if has_total else None
        for s in range(len(groups)):
            value = product(s, columns) if value is None else value + product(s, columns)
        if delta:
            depth = ups[0].shape[1]
            for o in range(replicas):
                value = value + jnp.dot(
                    spread[:, o * depth : (o + 1) * depth],
                    ups[o][0, :, columns],
                    preferred_element_type=f32,
                )
        if last:
            value = jnp.dot(hot[...], value.astype(bf16), preferred_element_type=f32)
        out[:, columns] = value.astype(out.dtype)

    width = out.shape[1]
    strip = min(strip_width, width) if last else width
    for start in range(0, width, strip):
        work(slice(start, start + strip))


def project(meta, ints, total, xs, weight, sizes, low=None, factors=None, rows=None, flops=1):
    replicas, capacity, pool = sizes
    columns = weight.shape[1]
    tile = min(column_tile, columns)
    in_specs = [smem] * 3
    args = list(ints)
    if total is not None:
        in_specs.append(pl.BlockSpec((live_total, tile), lambda i, m: (0, i)))
        args.append(total)
    for group in xs:
        for x in group:
            in_specs.append(pl.BlockSpec(x.shape, lambda i, m: (0, 0)))
            args.append(x)
    for s, group in enumerate(xs):
        k = group[0].shape[1]
        in_specs.append(pl.BlockSpec((k, tile), lambda i, m, s=s: (m[s], i)))
        args.append(weight)
    scratch = []
    if low is not None:
        in_specs.append(pl.BlockSpec(low.shape, lambda i, m: (0, 0)))
        args.append(low)
        depth = factors[0].shape[1]
        for u in factors:
            in_specs.append(pl.BlockSpec((1, depth, tile), lambda i, m: (1, 0, i)))
            args.append(u)
        scratch.append(pltpu.VMEM((live_total, replicas * depth), bf16))
    if rows is None:
        out = jax.ShapeDtypeStruct((live_total, columns), f32)
        out_spec = pl.BlockSpec((live_total, tile), lambda i, m: (0, i))
    else:
        out = jax.ShapeDtypeStruct((rows, columns), bf16)
        out_spec = pl.BlockSpec((rows, tile), lambda i, m: (0, i))
        scratch.append(pltpu.VMEM((rows, live_total), bf16))
    return pl.pallas_call(
        functools.partial(
            project_kernel,
            groups=tuple(len(g) for g in xs),
            has_total=total is not None,
            delta=low is not None,
            last=rows is not None,
            replicas=replicas,
            capacity=capacity,
            pool=pool,
        ),
        grid_spec=pltpu.PrefetchScalarGridSpec(
            num_scalar_prefetch=1,
            grid=(columns // tile,),
            in_specs=in_specs,
            out_specs=out_spec,
            scratch_shapes=scratch,
        ),
        out_shape=out,
        compiler_params=params(),
        cost_estimate=cost(flops),
        name="project",
    )(meta, *args)


def shards(
    hidden,
    query_weight,
    adapter_down,
    adapter_up,
    block_variant_index,
    variant_pool_slot,
    block_live_count,
):
    replicas = lax.axis_size("dp")
    tensor = lax.axis_size("tensor")
    place = lax.axis_index("tensor")
    pool = adapter_down.shape[0]
    blocks = block_variant_index.shape[1]
    rows, width = hidden.shape
    capacity = (blocks + replicas - 1) // replicas
    piece = width // 2
    ints = (block_variant_index, variant_pool_slot, block_live_count)
    sizes = (replicas, capacity, pool)

    def after(values, *events):
        return lax.optimization_barrier((values, events))[0]

    def add(total, items, **more):
        xs = [item[2] for item in items]
        meta = [item[0] * (width // item[2][0].shape[1]) + item[1] for item in items]
        meta = jnp.stack([jnp.asarray(m, i32) for m in meta])
        return project(meta, ints, total, xs, query_weight, sizes, **more)

    pools = (hidden, adapter_down, adapter_up)
    own0, (next_factors,) = prepare(ints, *pools, 0, 2, (1,), replicas, capacity)
    steps = (0,) + tuple(range(2, replicas))
    own1, factors = prepare(ints, *pools, 1, 2, steps, replicas, capacity)
    factors = [factors[0], next_factors, *factors[1:]]
    own = (own0, own1)

    def send(x, step):
        pairs = [(i, (i + step) % replicas) for i in range(replicas)]
        return lax.ppermute(x, "dp", pairs)

    own_total = add(None, [(place, j, (own[j],)) for j in range(2)])
    got = [factors[0], send(factors[1], 1)]
    for step in range(2, replicas):
        events = got[-1:] if step < replicas - 1 else [got[-1], own_total]
        got.append(send(after(factors[step], *events), step))

    if tensor != 4:
        gathered = [lax.all_gather(x, "tensor", axis=0) for x in own]
        low = lax.psum(shrink(*ints, own, got, capacity, pool), "tensor")
        low = low.astype(bf16).astype(f32).T
        total = own_total
        for step in range(1, tensor):
            device = (place + step) % tensor
            xs = [lax.dynamic_index_in_dim(x, device, 0, keepdims=False) for x in gathered]
            items = [(device, j, (xs[j],)) for j in range(2)]
            more = {"rows": rows, "low": low, "factors": got} if step == tensor - 1 else {}
            total = add(total, items, **more)
        return total

    def pairs(x):
        return lax.ppermute(x, "tensor", [(0, 1), (1, 0), (2, 3), (3, 2)])

    def middle(x):
        return lax.ppermute(x, "tensor", [(1, 2), (2, 1)])

    def outward(x):
        return lax.ppermute(x, "tensor", [(1, 0), (2, 3)])

    near = place ^ 1
    far = jnp.where(place < 2, 2, 1)
    farthest = jnp.where(place < 2, 3, 0)

    x1 = [pairs(x) for x in own]
    y1 = [middle(x) for x in own]
    near_total = add(own_total, [(near, 0, (x1[0],))])
    total = add(near_total, [(near, 1, (x1[1],))])
    partial = shrink(*ints[:2], after(ints[2], total), own, got, capacity, pool)

    x2_0, y2_0 = outward(y1[0]), middle(x1[0])
    x2_1, y2_1 = outward(after(y1[1], near_total)), middle(after(x1[1], near_total))
    total = add(total, [(far, 0, (y1[0], x2_0))], flops=3_450_000_000)

    inward = lax.ppermute(partial, "tensor", [(0, 1), (3, 2)])
    across = middle(partial + inward)
    across = after(across, y2_0)
    hopped = partial + across
    outer = outward(hopped)
    low = (partial + inward + across + outer).astype(bf16).astype(f32).T

    x3_0 = outward(after(y2_0, partial))
    y2_1 = after(y2_1, hopped, total)
    half = piece // 2
    halves = [y2_1[:, :half], y2_1[:, half:]]
    x3_1 = [outward(h) for h in halves]

    items = [(far, 1, (y1[1], x2_1)), (farthest, 0, (y2_0, x3_0))]
    total = add(total, items, low=low, factors=got, flops=2_300_000_000)
    total = add(total, [(farthest, 2, (halves[0], x3_1[0]))], flops=1_150_000_000)
    return add(total, [(farthest, 3, (halves[1], x3_1[1]))], rows=rows)


def solution(mesh):
    return jax.shard_map(
        shards,
        mesh=mesh,
        in_specs=(
            P(("groups", "dp"), "tensor"),
            P(None, "tensor"),
            P("dp", None, "tensor"),
            P("dp", None, "tensor"),
            P("groups", None),
            P("groups"),
            P(("groups", "dp"), None),
        ),
        out_specs=P(("groups", "dp"), "tensor"),
        check_vma=False,
    )
```

```python
import functools

import jax
import jax.numpy as jnp
from jax import lax
from jax.experimental import pallas as pl
from jax.experimental.pallas import tpu as pltpu
from jax.sharding import PartitionSpec as P

adapter_scale = 2.0
live_total = 576
column_tile = 512
pack_strip = 512
bf16, f32, i32 = jnp.bfloat16, jnp.float32, jnp.int32

smem = pl.BlockSpec(memory_space=pltpu.SMEM)
hbm = pl.BlockSpec(memory_space=pl.ANY)


def params(limit=62):
    return pltpu.CompilerParams(vmem_limit_bytes=limit * 1024 * 1024)


def cost(flops=1):
    return pl.CostEstimate(flops=flops, bytes_accessed=1, transcendentals=0)


def one_hot(live, rows, axis):
    blocks = live.shape[1]
    block = rows // blocks
    flat = (1, rows) if axis else (rows, 1)
    row = lax.broadcasted_iota(i32, flat, axis)
    place = jnp.full(flat, -1, i32)
    start = 0
    for b in range(blocks):
        inside = row - b * block
        here = (inside >= 0) & (inside < live[0, b])
        place = jnp.where(here, inside + start, place)
        start = start + live[0, b]
    shape = (live_total, rows) if axis else (rows, live_total)
    return (lax.broadcasted_iota(i32, shape, 1 - axis) == place).astype(f32).astype(bf16)


def prepare_kernel(
    variants, slots, live, x, down, up, packed, *rest, steps, replicas, capacity, blocks
):
    picked, hot, sems = rest[:-2], rest[-2], rest[-1]
    pool, rank = down.shape[0], down.shape[1]

    def copies():
        me = lax.axis_index("dp")
        made = []
        for step, place in zip(steps, picked):
            target = lax.rem(me + step, replicas)
            seen = jnp.int32(0)
            index = [jnp.int32(0)] * capacity
            for b in range(blocks):
                slot = slots[variants[target, b]]
                owner = lax.div(slot, pool)
                mine = owner == me
                for m in range(capacity):
                    index[m] = jnp.where(mine & (seen == m), slot - owner * pool, index[m])
                seen = seen + mine.astype(i32)
            for m in range(capacity):
                for kind, pooled in enumerate((down, up)):
                    made.append(
                        pltpu.make_async_copy(
                            pooled.at[index[m]],
                            place.at[kind, m * rank : (m + 1) * rank],
                            sems.at[len(made)],
                        )
                    )
        return made

    @pl.when(pl.program_id(0) == 0)
    def _():
        for copy in copies():
            copy.start()
        hot[...] = one_hot(live, x.shape[0], 1)

    packed[...] = jnp.dot(hot[...], x[...], preferred_element_type=f32).astype(bf16)

    @pl.when(pl.program_id(0) == pl.num_programs(0) - 1)
    def _():
        for copy in copies():
            copy.wait()


def prepare(ints, hidden, down, up, part, parts, steps, replicas, capacity):
    rows, features = hidden.shape
    width = features // parts
    strip = min(pack_strip, width)
    strips = width // strip
    depth = capacity * down.shape[1]
    outs = [jax.ShapeDtypeStruct((live_total, width), bf16)]
    outs += [jax.ShapeDtypeStruct((2, depth, features), bf16)] * len(steps)
    results = pl.pallas_call(
        functools.partial(
            prepare_kernel,
            steps=steps,
            replicas=replicas,
            capacity=capacity,
            blocks=ints[0].shape[1],
        ),
        grid=(strips,),
        in_specs=[smem] * 3 + [pl.BlockSpec((rows, strip), lambda i: (0, part * strips + i)), hbm, hbm],
        out_specs=[pl.BlockSpec((live_total, strip), lambda i: (0, i))]
        + [pl.BlockSpec(o.shape, lambda i: (0, 0, 0)) for o in outs[1:]],
        out_shape=outs,
        scratch_shapes=[
            pltpu.VMEM((live_total, rows), bf16),
            pltpu.SemaphoreType.DMA((len(steps) * capacity * 2,)),
        ],
        compiler_params=params(),
        cost_estimate=cost(),
        name="prepare",
    )(*ints, hidden, down, up)
    return results[0], results[1:]


def row_groups(variants, slots, live, shape, axis, replicas, capacity, pool):
    me = lax.axis_index("dp")
    blocks = live.shape[1]
    row = lax.broadcasted_iota(i32, shape, axis)
    group = jnp.zeros(shape, i32)
    start = 0
    owners = []
    for b in range(blocks):
        owner = lax.div(slots[variants[me, b]], pool)
        nth = sum([(o == owner).astype(i32) for o in owners], jnp.int32(0))
        owners.append(owner)
        mine = lax.rem(me - owner + replicas, replicas) * capacity + nth
        group = jnp.where(row >= start, mine, group)
        start = start + live[0, b]
    return group


def shrink_kernel(variants, slots, live, *rest, replicas, capacity, pool, chunks):
    xs, downs, out = rest[:chunks], rest[chunks : chunks + replicas], rest[-1]
    depth = downs[0].shape[1]
    rank = out.shape[0]
    shape = (depth, live_total)
    group = row_groups(variants, slots, live, shape, 1, replicas, capacity, pool)
    nth = lax.broadcasted_iota(i32, shape, 0) // rank
    total = jnp.zeros(shape, f32)
    for o in range(replicas):
        part = jnp.zeros(shape, f32)
        start = 0
        for x in xs:
            stop = start + x.shape[1]
            part = part + lax.dot_general(
                downs[o][0, :, start:stop],
                x[...],
                (((1,), (1,)), ((), ())),
                preferred_element_type=f32,
            )
            start = stop
        total = total + jnp.where(group == o * capacity + nth, part, 0.0)
    result = total[:rank]
    for m in range(1, capacity):
        result = result + total[m * rank : (m + 1) * rank]
    out[...] = result


def shrink(variants, slots, live, xs, factors, capacity, pool):
    replicas = len(factors)
    depth, width = factors[0].shape[1:]
    rank = depth // capacity
    whole = pl.BlockSpec(memory_space=pltpu.VMEM)
    down = pl.BlockSpec((1, depth, width), lambda i: (0, 0, 0))
    return pl.pallas_call(
        functools.partial(
            shrink_kernel, replicas=replicas, capacity=capacity, pool=pool, chunks=len(xs)
        ),
        grid=(1,),
        in_specs=[smem] * 3
        + [pl.BlockSpec(x.shape, lambda i: (0, 0)) for x in xs]
        + [down] * replicas,
        out_specs=pl.BlockSpec((rank, live_total), lambda i: (0, 0)),
        out_shape=jax.ShapeDtypeStruct((rank, live_total), f32),
        compiler_params=params(),
        cost_estimate=cost(),
        name="shrink",
    )(variants, slots, live, *xs, *factors)


def project_kernel(*refs, groups, widths, has_total, delta, last, replicas, capacity, pool):
    refs = list(refs)
    meta, variants, slots, live = refs[:4]
    refs = refs[4:]
    total = refs.pop(0) if has_total else None
    xs = [[refs.pop(0) for _ in range(g)] for g in groups]
    ws = [refs.pop(0) for _ in groups]
    low = refs.pop(0) if delta else None
    ups = [refs.pop(0) for _ in range(replicas)] if delta else None
    out = refs.pop(0)
    spread = refs.pop(0) if delta else None
    hot = refs.pop(0) if last else None

    if delta or last:

        @pl.when(pl.program_id(0) == 0)
        def _():
            if last:
                hot[...] = one_hot(live, out.shape[0], 0)
            if delta:
                depth = ups[0].shape[1]
                shape = (live_total, depth)
                group = row_groups(variants, slots, live, shape, 0, replicas, capacity, pool)
                nth = lax.broadcasted_iota(i32, shape, 1) // (depth // capacity)
                mine = low[...]
                rank = mine.shape[1]
                riding = xs[0][-1]
                for k in range(widths[0], riding.shape[1], rank):
                    mine = mine + riding[:, k : k + rank].astype(f32)
                mine = mine.astype(bf16).astype(f32)
                wide = jnp.concatenate([mine] * capacity, axis=1) * adapter_scale
                for o in range(replicas):
                    mine = jnp.where(group == o * capacity + nth, wide, 0.0)
                    spread[:, o * depth : (o + 1) * depth] = mine.astype(bf16)

    def product(s, columns):
        x = xs[s][0][:, : widths[s]]
        for other in xs[s][1:]:
            x = x + other[:, : widths[s]]
        return jnp.dot(x, ws[s][:, columns], preferred_element_type=f32)

    def work(columns):
        value = total[:, columns] if has_total else None
        for s in range(len(groups)):
            value = product(s, columns) if value is None else value + product(s, columns)
        if delta:
            depth = ups[0].shape[1]
            for o in range(replicas):
                value = value + jnp.dot(
                    spread[:, o * depth : (o + 1) * depth],
                    ups[o][0, :, columns],
                    preferred_element_type=f32,
                )
        if last:
            value = jnp.dot(hot[...], value.astype(bf16), preferred_element_type=f32)
        out[:, columns] = value.astype(out.dtype)

    work(slice(0, out.shape[1]))


def project(meta, ints, total, xs, widths, weight, sizes, low=None, factors=None, rows=None, flops=1, limit=62):
    replicas, capacity, pool = sizes
    columns = weight.shape[1]
    tile = min(column_tile, columns)
    in_specs = [smem] * 3
    args = list(ints)
    if total is not None:
        in_specs.append(pl.BlockSpec((live_total, tile), lambda i, m: (0, i)))
        args.append(total)
    for group in xs:
        for x in group:
            in_specs.append(pl.BlockSpec(x.shape, lambda i, m: (0, 0)))
            args.append(x)
    for s, group in enumerate(xs):
        k = widths[s]
        in_specs.append(pl.BlockSpec((k, tile), lambda i, m, s=s: (m[s], i)))
        args.append(weight)
    scratch = []
    if low is not None:
        in_specs.append(pl.BlockSpec(low.shape, lambda i, m: (0, 0)))
        args.append(low)
        depth = factors[0].shape[1]
        for u in factors:
            in_specs.append(pl.BlockSpec((1, depth, tile), lambda i, m: (1, 0, i)))
            args.append(u)
        scratch.append(pltpu.VMEM((live_total, replicas * depth), bf16))
    if rows is None:
        out = jax.ShapeDtypeStruct((live_total, columns), f32)
        out_spec = pl.BlockSpec((live_total, tile), lambda i, m: (0, i))
    else:
        out = jax.ShapeDtypeStruct((rows, columns), bf16)
        out_spec = pl.BlockSpec((rows, tile), lambda i, m: (0, i))
        scratch.append(pltpu.VMEM((rows, live_total), bf16))
    return pl.pallas_call(
        functools.partial(
            project_kernel,
            groups=tuple(len(g) for g in xs),
            widths=widths,
            has_total=total is not None,
            delta=low is not None,
            last=rows is not None,
            replicas=replicas,
            capacity=capacity,
            pool=pool,
        ),
        grid_spec=pltpu.PrefetchScalarGridSpec(
            num_scalar_prefetch=1,
            grid=(columns // tile,),
            in_specs=in_specs,
            out_specs=out_spec,
            scratch_shapes=scratch,
        ),
        out_shape=out,
        compiler_params=params(limit),
        cost_estimate=cost(flops),
        name="project",
    )(meta, *args)


def shards(
    hidden,
    query_weight,
    adapter_down,
    adapter_up,
    block_variant_index,
    variant_pool_slot,
    block_live_count,
):
    replicas = lax.axis_size("dp")
    tensor = lax.axis_size("tensor")
    place = lax.axis_index("tensor")
    pool = adapter_down.shape[0]
    blocks = block_variant_index.shape[1]
    rows, width = hidden.shape
    capacity = (blocks + replicas - 1) // replicas
    piece = width // 2
    ints = (block_variant_index, variant_pool_slot, block_live_count)
    sizes = (replicas, capacity, pool)

    def after(values, *events):
        return lax.optimization_barrier((values, events))[0]

    def add(total, items, **more):
        xs = [item[2] for item in items]
        widths = tuple(width // item[3] for item in items)
        meta = [item[0] * item[3] + item[1] for item in items]
        meta = jnp.stack([jnp.asarray(m, i32) for m in meta])
        return project(meta, ints, total, xs, widths, query_weight, sizes, **more)

    pools = (hidden, adapter_down, adapter_up)
    own0, (next_factors,) = prepare(ints, *pools, 0, 2, (1,), replicas, capacity)
    steps = (0,) + tuple(range(2, replicas))
    own1, factors = prepare(ints, *pools, 1, 2, steps, replicas, capacity)
    factors = [factors[0], next_factors, *factors[1:]]
    own = (own0, own1)

    def send(x, step):
        pairs = [(i, (i + step) % replicas) for i in range(replicas)]
        return lax.ppermute(x, "dp", pairs)

    own_total = add(None, [(place, j, (own[j],), 2) for j in range(2)])
    got = [factors[0], send(factors[1], 1)]
    for step in range(2, replicas):
        events = got[-1:] if step < replicas - 1 else [got[-1], own_total]
        got.append(send(after(factors[step], *events), step))

    if tensor != 4:
        gathered = [lax.all_gather(x, "tensor", axis=0) for x in own]
        low = lax.psum(shrink(*ints, own, got, capacity, pool), "tensor")
        low = low.T
        total = own_total
        for step in range(1, tensor):
            device = (place + step) % tensor
            xs = [lax.dynamic_index_in_dim(x, device, 0, keepdims=False) for x in gathered]
            items = [(device, j, (xs[j],), 2) for j in range(2)]
            more = {"rows": rows, "low": low, "factors": got} if step == tensor - 1 else {}
            total = add(total, items, **more)
        return total

    def pairs(x):
        return lax.ppermute(x, "tensor", [(0, 1), (1, 0), (2, 3), (3, 2)])

    def middle(x):
        return lax.ppermute(x, "tensor", [(1, 2), (2, 1)])

    def outward(x):
        return lax.ppermute(x, "tensor", [(1, 0), (2, 3)])

    near = place ^ 1
    far = jnp.where(place < 2, 2, 1)
    farthest = jnp.where(place < 2, 3, 0)

    x1 = [pairs(x) for x in own]
    y1 = [middle(x) for x in own]
    near_total = add(own_total, [(near, 0, (x1[0],), 2)])
    total = add(near_total, [(near, 1, (x1[1],), 2)])
    partial = shrink(*ints[:2], after(ints[2], total, y1[1]), own, got, capacity, pool)

    x2_0, y2_0 = outward(y1[0]), middle(x1[0])
    x2_1, y2_1 = outward(after(y1[1], near_total)), middle(after(x1[1], near_total))
    total = add(total, [(far, 0, (y1[0], x2_0), 2)], flops=3_450_000_000)

    inward = lax.ppermute(partial, "tensor", [(0, 1), (3, 2)])
    across = middle(partial + inward)
    across = after(across, y2_0)
    hopped = (partial + across).T
    low = (partial + inward + across).T

    x3_0 = outward(after(y2_0, partial))
    y2_1 = after(y2_1, hopped, total)
    half = piece // 2
    upper = hopped.astype(bf16)
    rest = (hopped - upper.astype(f32)).astype(bf16)
    first_half = jnp.concatenate([y2_1[:, :half], upper, rest], axis=1)
    halves = [first_half, after(y2_1, first_half)[:, half:]]
    x3_1 = [outward(h) for h in halves]

    items = [(far, 1, (y1[1], x2_1), 2), (farthest, 0, (y2_0, x3_0), 2)]
    total = add(total, items, flops=5_750_000_000)
    items = [(farthest, 2, (halves[0], x3_1[0]), 4)]
    total = add(total, items, low=low, factors=got, flops=1_150_000_000, limit=24)
    return add(total, [(farthest, 3, (halves[1], x3_1[1]), 4)], rows=rows, limit=24)


def solution(mesh):
    return jax.shard_map(
        shards,
        mesh=mesh,
        in_specs=(
            P(("groups", "dp"), "tensor"),
            P(None, "tensor"),
            P("dp", None, "tensor"),
            P("dp", None, "tensor"),
            P("groups", None),
            P("groups"),
            P(("groups", "dp"), None),
        ),
        out_specs=P(("groups", "dp"), "tensor"),
        check_vma=False,
    )
```

```python
import functools

import jax
import jax.numpy as jnp
from jax import lax
from jax.experimental import pallas as pl
from jax.experimental.pallas import tpu as pltpu
from jax.sharding import PartitionSpec as P

adapter_scale = 2.0
live_total = 576
column_tile = 512
pack_strip = 512
bf16, f32, i32 = jnp.bfloat16, jnp.float32, jnp.int32

smem = pl.BlockSpec(memory_space=pltpu.SMEM)
hbm = pl.BlockSpec(memory_space=pl.ANY)


def params(limit=62):
    return pltpu.CompilerParams(vmem_limit_bytes=limit * 1024 * 1024)


def cost(flops=1):
    return pl.CostEstimate(flops=flops, bytes_accessed=1, transcendentals=0)


def one_hot(live, rows, axis):
    blocks = live.shape[1]
    block = rows // blocks
    flat = (1, rows) if axis else (rows, 1)
    row = lax.broadcasted_iota(i32, flat, axis)
    place = jnp.full(flat, -1, i32)
    start = 0
    for b in range(blocks):
        inside = row - b * block
        here = (inside >= 0) & (inside < live[0, b])
        place = jnp.where(here, inside + start, place)
        start = start + live[0, b]
    shape = (live_total, rows) if axis else (rows, live_total)
    return (lax.broadcasted_iota(i32, shape, 1 - axis) == place).astype(f32).astype(bf16)


def prepare_kernel(
    variants, slots, live, x, down, up, packed, *rest, steps, replicas, capacity, blocks
):
    picked, hot, sems = rest[:-2], rest[-2], rest[-1]
    pool, rank = down.shape[0], down.shape[1]

    def copies():
        me = lax.axis_index("dp")
        made = []
        for step, place in zip(steps, picked):
            target = lax.rem(me + step, replicas)
            seen = jnp.int32(0)
            index = [jnp.int32(0)] * capacity
            for b in range(blocks):
                slot = slots[variants[target, b]]
                owner = lax.div(slot, pool)
                mine = owner == me
                for m in range(capacity):
                    index[m] = jnp.where(mine & (seen == m), slot - owner * pool, index[m])
                seen = seen + mine.astype(i32)
            for m in range(capacity):
                for kind, pooled in enumerate((down, up)):
                    made.append(
                        pltpu.make_async_copy(
                            pooled.at[index[m]],
                            place.at[kind, m * rank : (m + 1) * rank],
                            sems.at[len(made)],
                        )
                    )
        return made

    @pl.when(pl.program_id(0) == 0)
    def _():
        for copy in copies():
            copy.start()
        hot[...] = one_hot(live, x.shape[0], 1)

    packed[...] = jnp.dot(hot[...], x[...], preferred_element_type=f32).astype(bf16)

    @pl.when(pl.program_id(0) == pl.num_programs(0) - 1)
    def _():
        for copy in copies():
            copy.wait()


def prepare(ints, hidden, down, up, part, parts, steps, replicas, capacity):
    rows, features = hidden.shape
    width = features // parts
    strip = min(pack_strip, width)
    strips = width // strip
    depth = capacity * down.shape[1]
    outs = [jax.ShapeDtypeStruct((live_total, width), bf16)]
    outs += [jax.ShapeDtypeStruct((2, depth, features), bf16)] * len(steps)
    results = pl.pallas_call(
        functools.partial(
            prepare_kernel,
            steps=steps,
            replicas=replicas,
            capacity=capacity,
            blocks=ints[0].shape[1],
        ),
        grid=(strips,),
        in_specs=[smem] * 3 + [pl.BlockSpec((rows, strip), lambda i: (0, part * strips + i)), hbm, hbm],
        out_specs=[pl.BlockSpec((live_total, strip), lambda i: (0, i))]
        + [pl.BlockSpec(o.shape, lambda i: (0, 0, 0)) for o in outs[1:]],
        out_shape=outs,
        scratch_shapes=[
            pltpu.VMEM((live_total, rows), bf16),
            pltpu.SemaphoreType.DMA((len(steps) * capacity * 2,)),
        ],
        compiler_params=params(),
        cost_estimate=cost(),
        name="prepare",
    )(*ints, hidden, down, up)
    return results[0], results[1:]


def row_groups(variants, slots, live, shape, axis, replicas, capacity, pool):
    me = lax.axis_index("dp")
    blocks = live.shape[1]
    row = lax.broadcasted_iota(i32, shape, axis)
    group = jnp.zeros(shape, i32)
    start = 0
    owners = []
    for b in range(blocks):
        owner = lax.div(slots[variants[me, b]], pool)
        nth = sum([(o == owner).astype(i32) for o in owners], jnp.int32(0))
        owners.append(owner)
        mine = lax.rem(me - owner + replicas, replicas) * capacity + nth
        group = jnp.where(row >= start, mine, group)
        start = start + live[0, b]
    return group


def shrink_kernel(variants, slots, live, *rest, replicas, capacity, pool, chunks):
    xs, downs, out = rest[:chunks], rest[chunks : chunks + replicas], rest[-1]
    depth = downs[0].shape[1]
    rank = out.shape[0]
    shape = (depth, live_total)
    group = row_groups(variants, slots, live, shape, 1, replicas, capacity, pool)
    nth = lax.broadcasted_iota(i32, shape, 0) // rank
    total = jnp.zeros(shape, f32)
    for o in range(replicas):
        part = jnp.zeros(shape, f32)
        start = 0
        for x in xs:
            stop = start + x.shape[1]
            part = part + lax.dot_general(
                downs[o][0, :, start:stop],
                x[...],
                (((1,), (1,)), ((), ())),
                preferred_element_type=f32,
            )
            start = stop
        total = total + jnp.where(group == o * capacity + nth, part, 0.0)
    result = total[:rank]
    for m in range(1, capacity):
        result = result + total[m * rank : (m + 1) * rank]
    out[...] = result


def shrink(variants, slots, live, xs, factors, capacity, pool):
    replicas = len(factors)
    depth, width = factors[0].shape[1:]
    rank = depth // capacity
    whole = pl.BlockSpec(memory_space=pltpu.VMEM)
    down = pl.BlockSpec((1, depth, width), lambda i: (0, 0, 0))
    return pl.pallas_call(
        functools.partial(
            shrink_kernel, replicas=replicas, capacity=capacity, pool=pool, chunks=len(xs)
        ),
        grid=(1,),
        in_specs=[smem] * 3
        + [pl.BlockSpec(x.shape, lambda i: (0, 0)) for x in xs]
        + [down] * replicas,
        out_specs=pl.BlockSpec((rank, live_total), lambda i: (0, 0)),
        out_shape=jax.ShapeDtypeStruct((rank, live_total), f32),
        compiler_params=params(),
        cost_estimate=cost(),
        name="shrink",
    )(variants, slots, live, *xs, *factors)


def project_kernel(*refs, groups, widths, has_total, delta, last, replicas, capacity, pool):
    refs = list(refs)
    meta, variants, slots, live = refs[:4]
    refs = refs[4:]
    total = refs.pop(0) if has_total else None
    xs = [[refs.pop(0) for _ in range(g)] for g in groups]
    ws = [refs.pop(0) for _ in groups]
    low = refs.pop(0) if delta else None
    ups = [refs.pop(0) for _ in range(replicas)] if delta else None
    out = refs.pop(0)
    spread = refs.pop(0) if delta else None
    hot = refs.pop(0) if last else None

    if delta or last:

        @pl.when(pl.program_id(0) == 0)
        def _():
            if last:
                hot[...] = one_hot(live, out.shape[0], 0)
            if delta:
                depth = ups[0].shape[1]
                shape = (live_total, depth)
                group = row_groups(variants, slots, live, shape, 0, replicas, capacity, pool)
                nth = lax.broadcasted_iota(i32, shape, 1) // (depth // capacity)
                mine = low[...]
                rank = mine.shape[1]
                riding = xs[0][-1]
                for k in range(widths[0], riding.shape[1], rank):
                    mine = mine + riding[:, k : k + rank].astype(f32)
                mine = mine.astype(bf16).astype(f32)
                wide = jnp.concatenate([mine] * capacity, axis=1) * adapter_scale
                for o in range(replicas):
                    mine = jnp.where(group == o * capacity + nth, wide, 0.0)
                    spread[:, o * depth : (o + 1) * depth] = mine.astype(bf16)

    def product(s, columns):
        x = xs[s][0][:, : widths[s]]
        for other in xs[s][1:]:
            x = x + other[:, : widths[s]]
        return jnp.dot(x, ws[s][:, columns], preferred_element_type=f32)

    def work(columns):
        value = total[:, columns] if has_total else None
        for s in range(len(groups)):
            value = product(s, columns) if value is None else value + product(s, columns)
        if delta:
            depth = ups[0].shape[1]
            for o in range(replicas):
                value = value + jnp.dot(
                    spread[:, o * depth : (o + 1) * depth],
                    ups[o][0, :, columns],
                    preferred_element_type=f32,
                )
        if last:
            value = jnp.dot(hot[...], value.astype(bf16), preferred_element_type=f32)
        out[:, columns] = value.astype(out.dtype)

    work(slice(0, out.shape[1]))


def project(meta, ints, total, xs, widths, weight, sizes, low=None, factors=None, rows=None, flops=1, limit=62):
    replicas, capacity, pool = sizes
    columns = weight.shape[1]
    tile = min(column_tile, columns)
    in_specs = [smem] * 3
    args = list(ints)
    if total is not None:
        in_specs.append(pl.BlockSpec((live_total, tile), lambda i, m: (0, i)))
        args.append(total)
    for group in xs:
        for x in group:
            in_specs.append(pl.BlockSpec(x.shape, lambda i, m: (0, 0)))
            args.append(x)
    for s, group in enumerate(xs):
        k = widths[s]
        in_specs.append(pl.BlockSpec((k, tile), lambda i, m, s=s: (m[s], i)))
        args.append(weight)
    scratch = []
    if low is not None:
        in_specs.append(pl.BlockSpec(low.shape, lambda i, m: (0, 0)))
        args.append(low)
        depth = factors[0].shape[1]
        for u in factors:
            in_specs.append(pl.BlockSpec((1, depth, tile), lambda i, m: (1, 0, i)))
            args.append(u)
        scratch.append(pltpu.VMEM((live_total, replicas * depth), bf16))
    if rows is None:
        out = jax.ShapeDtypeStruct((live_total, columns), f32)
        out_spec = pl.BlockSpec((live_total, tile), lambda i, m: (0, i))
    else:
        out = jax.ShapeDtypeStruct((rows, columns), bf16)
        out_spec = pl.BlockSpec((rows, tile), lambda i, m: (0, i))
        scratch.append(pltpu.VMEM((rows, live_total), bf16))
    return pl.pallas_call(
        functools.partial(
            project_kernel,
            groups=tuple(len(g) for g in xs),
            widths=widths,
            has_total=total is not None,
            delta=low is not None,
            last=rows is not None,
            replicas=replicas,
            capacity=capacity,
            pool=pool,
        ),
        grid_spec=pltpu.PrefetchScalarGridSpec(
            num_scalar_prefetch=1,
            grid=(columns // tile,),
            in_specs=in_specs,
            out_specs=out_spec,
            scratch_shapes=scratch,
        ),
        out_shape=out,
        compiler_params=params(limit),
        cost_estimate=cost(flops),
        name="project",
    )(meta, *args)


def shards(
    hidden,
    query_weight,
    adapter_down,
    adapter_up,
    block_variant_index,
    variant_pool_slot,
    block_live_count,
):
    replicas = lax.axis_size("dp")
    tensor = lax.axis_size("tensor")
    place = lax.axis_index("tensor")
    pool = adapter_down.shape[0]
    blocks = block_variant_index.shape[1]
    rows, width = hidden.shape
    capacity = (blocks + replicas - 1) // replicas
    piece = width // 2
    ints = (block_variant_index, variant_pool_slot, block_live_count)
    sizes = (replicas, capacity, pool)

    def after(values, *events):
        return lax.optimization_barrier((values, events))[0]

    def add(total, items, **more):
        xs = [item[2] for item in items]
        widths = tuple(width // item[3] for item in items)
        meta = [item[0] * item[3] + item[1] for item in items]
        meta = jnp.stack([jnp.asarray(m, i32) for m in meta])
        return project(meta, ints, total, xs, widths, query_weight, sizes, **more)

    pools = (hidden, adapter_down, adapter_up)
    own0, (next_factors,) = prepare(ints, *pools, 0, 2, (1,), replicas, capacity)
    steps = (0,) + tuple(range(2, replicas))
    own1, factors = prepare(ints, *pools, 1, 2, steps, replicas, capacity)
    factors = [factors[0], next_factors, *factors[1:]]
    own = (own0, own1)

    def send(x, step):
        pairs = [(i, (i + step) % replicas) for i in range(replicas)]
        return lax.ppermute(x, "dp", pairs)

    own_total = add(None, [(place, j, (own[j],), 2) for j in range(2)])
    got = [factors[0], send(factors[1], 1)]
    for step in range(2, replicas):
        events = got[-1:] if step < replicas - 1 else [got[-1], own_total]
        got.append(send(after(factors[step], *events), step))

    if tensor != 4:
        gathered = [lax.all_gather(x, "tensor", axis=0) for x in own]
        low = lax.psum(shrink(*ints, own, got, capacity, pool), "tensor")
        low = low.T
        total = own_total
        for step in range(1, tensor):
            device = (place + step) % tensor
            xs = [lax.dynamic_index_in_dim(x, device, 0, keepdims=False) for x in gathered]
            items = [(device, j, (xs[j],), 2) for j in range(2)]
            more = {"rows": rows, "low": low, "factors": got} if step == tensor - 1 else {}
            total = add(total, items, **more)
        return total

    def pairs(x):
        return lax.ppermute(x, "tensor", [(0, 1), (1, 0), (2, 3), (3, 2)])

    def middle(x):
        return lax.ppermute(x, "tensor", [(1, 2), (2, 1)])

    def outward(x):
        return lax.ppermute(x, "tensor", [(1, 0), (2, 3)])

    near = place ^ 1
    far = jnp.where(place < 2, 2, 1)
    farthest = jnp.where(place < 2, 3, 0)

    x1 = [pairs(x) for x in own]
    y1 = [middle(x) for x in own]
    near_total = add(own_total, [(near, 0, (x1[0],), 2)])
    total = add(near_total, [(near, 1, (x1[1],), 2)])
    partial = shrink(*ints[:2], after(ints[2], total, y1[1]), own, got, capacity, pool)

    x2_0, y2_0 = outward(y1[0]), middle(x1[0])
    x2_1, y2_1 = outward(after(y1[1], near_total)), middle(after(x1[1], near_total))
    total = add(total, [(far, 0, (y1[0], x2_0), 2)], flops=3_450_000_000)

    inward = lax.ppermute(partial, "tensor", [(0, 1), (3, 2)])
    across = middle(partial + inward)
    across = after(across, y2_0)
    hopped = (partial + across).T
    low = (partial + inward + across).T

    x3_0 = outward(after(y2_0, partial))
    y2_1 = after(y2_1, hopped, total)
    half = piece // 2
    upper = lax.optimization_barrier(hopped.astype(bf16))
    rest = (hopped - upper.astype(f32)).astype(bf16)
    first_half = jnp.concatenate([y2_1[:, :half], upper, rest], axis=1)
    halves = [first_half, after(y2_1, first_half)[:, half:]]
    x3_1 = [outward(h) for h in halves]

    items = [(far, 1, (y1[1], x2_1), 2), (farthest, 0, (y2_0, x3_0), 2)]
    total = add(total, items, flops=10_350_000_000)
    items = [(farthest, 2, (halves[0], x3_1[0]), 4)]
    total = add(total, items, low=low, factors=got, flops=1_150_000_000, limit=24)
    return add(total, [(farthest, 3, (halves[1], x3_1[1]), 4)], rows=rows, limit=24)


def solution(mesh):
    return jax.shard_map(
        shards,
        mesh=mesh,
        in_specs=(
            P(("groups", "dp"), "tensor"),
            P(None, "tensor"),
            P("dp", None, "tensor"),
            P("dp", None, "tensor"),
            P("groups", None),
            P("groups"),
            P(("groups", "dp"), None),
        ),
        out_specs=P(("groups", "dp"), "tensor"),
        check_vma=False,
    )
```
